256 devices in a mesh: gx: 16 (over z, x_lo), gy: 4 (over y), gz: 4 (over x_hi, core).
Axes of the slice: x: 4 (x_hi: 2, x_lo: 2; x = x_hi * 2 + x_lo), y: 4, z: 8, core: 2. Of those that a mesh axis runs over, the one named last changes fastest.
Arguments:
- loads: float32 [16, 1048576], P(None, ('gx', 'gy', 'gz')), may hold values from -50 to 50
- displacement: float32 [1048576], P(('gx', 'gy', 'gz')), may hold values from -6 to 6
- stiffness: float32 [16384, 7, 4096], P(('gx', 'gy', 'gz')), may hold values from -100 to 300, as said below
- col_index: int32 [16384, 7], P(('gx', 'gy', 'gz')), may hold values from 0 to 159, as said below
- face_index: int32 [1536, 16], P(('gx', 'gy', 'gz')), may hold values from 0 to 63, as said below
- zone_map: int32 [16384, 6], P(('gx', 'gy', 'gz')), may hold values from 0 to 32767, as said below
Outputs:
- adjoint: float32 [16, 1048576], P(None, ('gx', 'gy', 'gz'))
- sensitivity: float32 [16, 32768], P(None, ('gx', 'gy', 'gz'))
The draws below stay inside these ranges and needn't reach their ends.
Inputs may be any that keep to these rules, and one draw needn't show every extreme that they name: `col_index`: in each aligned block of 64 rows (one subdomain), entry 0 of row r is r, and entries 1 to 6 name the row's coupled node blocks in directions -x, +x, -y, +y, -z, +z: one of the same subdomain by its row within the block, one across a face by 64 + d * 16 + f, f being the row's position in that subdomain's face list for direction d. Block at position f of a face in direction d touches the block at position f of the neighbour's face in the opposite direction. `face_index`: row 6 * s + d lists, each once, the subdomain's node blocks (rows within its block of 64) on its face in direction d. `zone_map`: entries of subdomain s lie in zones s * 128 to s * 128 + 2 * 128 - 1, taken modulo 32768; both ends of this window occur in every subdomain. `stiffness`: the whole operator is symmetric positive definite; diagonal entries of the diagonal blocks are positive.
All inputs are finite; a program needn't handle non-finite values.
Results may differ from the reference program's by a relative error of at most 0.0003.
Values sent between devices are 32-bit elements; how exact they have to be, the bound alone decides.
A program may use at most 128 MiB of HBM per device.

```python
import jax
import jax.numpy as jnp
from jax import lax

BSIDE = 4
BDOF = 64
OUTS = 16
ITERS = 2
ZONE_DEV = 128
NBLK = 64
FACE = 16
SUB_X = 16
SUB_Y = 4
SUB_Z = 4
SUBDOMAINS = 256
BLOCKS = 16384
DOFS = 1048576
ZONES = 32768


def subdomain_perms(key):
    base_key = jax.random.fold_in(key, 11)

    def one_perm(sub_id):
        return jax.random.permutation(jax.random.fold_in(base_key, sub_id), NBLK).astype(jnp.int32)
    return jax.vmap(one_perm)(jnp.arange(SUBDOMAINS, dtype=jnp.int32))


def grid_coords():
    cell_ids = jnp.arange(NBLK, dtype=jnp.int32)
    return (cell_ids // (BSIDE * BSIDE), cell_ids // BSIDE % BSIDE, cell_ids % BSIDE)


def neighbour_table(perm):
    first, second, third = grid_coords()
    coord_list = [first, second, third]
    face_pos = [second * BSIDE + third, first * BSIDE + third, first * BSIDE + second]
    columns = [perm]
    for direction in range(6):
        axis_id = direction // 2
        offset = 1 if direction % 2 == 1 else -1
        moved = [coord_list[0], coord_list[1], coord_list[2]]
        moved[axis_id] = moved[axis_id] + offset
        inside = (moved[axis_id] >= 0) & (moved[axis_id] < BSIDE)
        clipped = [jnp.clip(moved[0], 0, BSIDE - 1), jnp.clip(moved[1], 0, BSIDE - 1), jnp.clip(moved[2], 0, BSIDE - 1)]
        target = (clipped[0] * BSIDE + clipped[1]) * BSIDE + clipped[2]
        outside_id = NBLK + direction * FACE + face_pos[axis_id]
        columns.append(jnp.where(inside, perm[target], outside_id).astype(jnp.int32))
    table = jnp.stack(columns, axis=1)
    return jnp.zeros_like(table).at[perm].set(table)


def face_table(perm):
    spots = jnp.arange(FACE, dtype=jnp.int32)
    high_part = spots // BSIDE
    low_part = spots % BSIDE
    last = BSIDE - 1
    cells = jnp.stack([spots, last * FACE + spots, high_part * FACE + low_part, high_part * FACE + last * BSIDE + low_part, spots * BSIDE, spots * BSIDE + last], axis=0)
    return perm[cells]


def draw_col_index(key, part):
    perms = subdomain_perms(key)
    return jax.vmap(neighbour_table)(perms).reshape(BLOCKS, 7)


def draw_face_index(key, part):
    perms = subdomain_perms(key)
    return jax.vmap(face_table)(perms).reshape(SUBDOMAINS * 6, FACE)


def draw_stiffness(key, part):
    perms = subdomain_perms(key)
    edge_key = jax.random.fold_in(key, 23)
    node_key = jax.random.fold_in(key, 29)
    weight_lo, weight_hi, shift_lo, shift_hi = (0.25, 2.5, 0.3, 3.0)
    spans = [SUB_X * BSIDE + 1, SUB_Y * BSIDE + 1, SUB_Z * BSIDE + 1]

    def coupling(edge_id):
        inner_key = jax.random.fold_in(edge_key, edge_id)
        factor = jnp.clip(jax.random.normal(inner_key, (BDOF, BDOF), jnp.float32), -6.0, 6.0)
        weight = jnp.exp(jax.random.uniform(jax.random.fold_in(inner_key, 1), (), jnp.float32, jnp.log(weight_lo), jnp.log(weight_hi)))
        return weight * jnp.dot(factor, factor.T, precision=lax.Precision.HIGHEST) / BDOF

    def node_shift(node_id):
        return jnp.exp(jax.random.uniform(jax.random.fold_in(node_key, node_id), (BDOF,), jnp.float32, jnp.log(shift_lo), jnp.log(shift_hi)))

    def one_sub(pair):
        sub_id, perm = pair
        first, second, third = grid_coords()
        glob = [sub_id // (SUB_Y * SUB_Z) * BSIDE + first, sub_id // SUB_Z % SUB_Y * BSIDE + second, sub_id % SUB_Z * BSIDE + third]
        pieces = []
        for direction in range(6):
            axis_id = direction // 2
            edge_pos = [glob[0], glob[1], glob[2]]
            edge_pos[axis_id] = edge_pos[axis_id] + direction % 2
            edge_id = ((axis_id * spans[0] + edge_pos[0]) * spans[1] + edge_pos[1]) * spans[2] + edge_pos[2]
            pieces.append(jax.vmap(coupling)(edge_id.astype(jnp.int32)))
        couplings = jnp.stack(pieces, axis=1)
        node_id = (glob[0] * (SUB_Y * BSIDE) + glob[1]) * (SUB_Z * BSIDE) + glob[2]
        shifts = jax.vmap(node_shift)(node_id.astype(jnp.int32))
        diag_block = jax.vmap(jnp.diag)(shifts) + jnp.sum(couplings, axis=1)
        table = jnp.concatenate([diag_block[:, None], -couplings], axis=1).reshape(NBLK, 7, BDOF * BDOF)
        return jnp.zeros_like(table).at[perm].set(table)
    values = lax.map(one_sub, (jnp.arange(SUBDOMAINS, dtype=jnp.int32), perms))
    return values.reshape(BLOCKS, 7, BDOF * BDOF).astype(jnp.float32)


def draw_zone_map(key, part):
    width = NBLK * 6
    offsets = jax.random.randint(jax.random.fold_in(key, 31), (SUBDOMAINS, width), 0, 2 * ZONE_DEV, jnp.int32)
    high_spot = jax.random.randint(jax.random.fold_in(key, 37), (SUBDOMAINS,), 0, width, jnp.int32)
    gap_spot = jax.random.randint(jax.random.fold_in(key, 41), (SUBDOMAINS,), 1, width, jnp.int32)
    low_spot = (high_spot + gap_spot) % width
    sub_ids = jnp.arange(SUBDOMAINS, dtype=jnp.int32)
    offsets = offsets.at[sub_ids, high_spot].set(2 * ZONE_DEV - 1)
    offsets = offsets.at[sub_ids, low_spot].set(0)
    zones_all = (sub_ids[:, None] * ZONE_DEV + offsets) % ZONES
    return zones_all.reshape(BLOCKS, 6).astype(jnp.int32)


def draw_loads(key, part):
    sub_of = jnp.arange(DOFS, dtype=jnp.int32) // (NBLK * BDOF)
    sub_scale = jnp.exp(jnp.log(3.0) * sub_of.astype(jnp.float32) / (SUBDOMAINS - 1))
    col_scale = jnp.exp(jax.random.uniform(jax.random.fold_in(key, 2), (OUTS, 1), jnp.float32, 0.0, jnp.log(10.0))) / 3.0
    base = jnp.clip(jax.random.normal(jax.random.fold_in(key, 3), (OUTS, DOFS), jnp.float32), -5.0, 5.0)
    return (base * col_scale * sub_scale[None, :]).astype(jnp.float32)


def level_of(key, shape, split, least, high):
    level, own = 1.0, jax.random.fold_in(key, 6)
    for axis_at, blocks in split:
        heights = jnp.exp(jax.random.uniform(jax.random.fold_in(own, axis_at), (blocks,), jnp.float32, least / len(split), high / len(split)))
        level = level * jnp.repeat(heights, shape[axis_at] // blocks).reshape([-1 if axis == axis_at else 1 for axis in range(len(shape))])
    return level


def noise(own_key, dims, deviation, reach, split=(), kind=jnp.bfloat16):
    array = jax.random.normal(own_key, dims, jnp.float32) * deviation
    if len(split) > 0:
        array = level_of(own_key, dims, split, -0.22, 0.18) * array
    return jnp.clip(array, min=-reach, max=reach).astype(kind)


def setup_inputs(seed: int = 0) -> dict:
    key_of = jax.random.split(jax.random.key(seed), 7)
    return {
        "loads": draw_loads(jax.random.fold_in(key_of[6], 71), 0),
        "displacement": noise(key_of[1], (DOFS,), 1.0, 6.0, ((0, 256),), jnp.float32),
        "stiffness": draw_stiffness(jax.random.fold_in(key_of[6], 71), 0),
        "col_index": draw_col_index(jax.random.fold_in(key_of[6], 71), 0),
        "face_index": draw_face_index(jax.random.fold_in(key_of[6], 71), 0),
        "zone_map": draw_zone_map(jax.random.fold_in(key_of[6], 71), 0),
    }


def halo_from(grid_side, axis_id, from_low):
    pads = [(0, 0)] * grid_side.ndim
    pads[axis_id] = (1, 0) if from_low else (0, 1)
    padded = jnp.pad(grid_side, pads)
    begin = 0 if from_low else 1
    return lax.slice_in_dim(padded, begin, begin + grid_side.shape[axis_id], axis=axis_id)

def pick_faces(cube_in, face_list):
    return cube_in[:, face_list]

def pick_cols(extended, col_list):
    return extended[:, col_list]

def extend_all(field_in, face_index):
    height = field_in.shape[0]
    cubes = field_in.reshape(height, SUBDOMAINS, NBLK, BDOF).transpose(1, 0, 2, 3)
    lists = face_index.reshape(SUBDOMAINS, 6, FACE)
    picked = jax.vmap(pick_faces)(cubes, lists)
    grid = picked.reshape(SUB_X, SUB_Y, SUB_Z, height, 6, FACE, BDOF)
    sides = [halo_from(grid[:, :, :, :, 1], 0, True), halo_from(grid[:, :, :, :, 0], 0, False), halo_from(grid[:, :, :, :, 3], 1, True), halo_from(grid[:, :, :, :, 2], 1, False), halo_from(grid[:, :, :, :, 5], 2, True), halo_from(grid[:, :, :, :, 4], 2, False)]
    halos = jnp.stack(sides, axis=4).reshape(SUBDOMAINS, height, 6 * FACE, BDOF)
    return jnp.concatenate([cubes, halos], axis=2)

def apply_all(field_in, blocks, col_index, face_index):
    extended = extend_all(field_in, face_index)
    col_lists = col_index.reshape(SUBDOMAINS, NBLK, 7)
    gathered = jax.vmap(pick_cols)(extended, col_lists)
    image = jnp.einsum('nakij,ncakj->ncai', blocks, gathered, precision=lax.Precision.HIGHEST)
    return image.transpose(1, 0, 2, 3).reshape(field_in.shape[0], DOFS)

def inner_gram(left_in, right_in):
    return jnp.dot(left_in, right_in.T, precision=lax.Precision.HIGHEST)

def cho_apply(matrix_in, right_in):
    factor = jnp.linalg.cholesky(matrix_in)
    return jax.scipy.linalg.cho_solve((factor, True), right_in)

def reference(loads, displacement, stiffness, col_index, face_index, zone_map):
    blocks = stiffness.reshape(SUBDOMAINS, NBLK, 7, BDOF, BDOF)
    inverse_diag = (1.0 / jnp.diagonal(blocks[:, :, 0], axis1=2, axis2=3)).reshape(DOFS)
    adjoint = jnp.zeros_like(loads)
    residual = loads
    precond = residual * inverse_diag[None, :]
    direction = precond
    norm_gram = inner_gram(residual, precond)
    for step in range(ITERS):
        image = apply_all(direction, blocks, col_index, face_index)
        curvature = inner_gram(direction, image)
        step_size = cho_apply(curvature, norm_gram)
        adjoint = adjoint + jnp.dot(step_size.T, direction, precision=lax.Precision.HIGHEST)
        residual = residual - jnp.dot(step_size.T, image, precision=lax.Precision.HIGHEST)
        if step + 1 < ITERS:
            precond = residual * inverse_diag[None, :]
            next_gram = inner_gram(residual, precond)
            mix_ratio = cho_apply(norm_gram, next_gram)
            direction = precond + jnp.dot(mix_ratio.T, direction, precision=lax.Precision.HIGHEST)
            norm_gram = next_gram
    stacked = jnp.concatenate([adjoint, displacement[None, :]], axis=0)
    extended = extend_all(stacked, face_index)
    col_lists = col_index.reshape(SUBDOMAINS, NBLK, 7)
    beside = jax.vmap(pick_cols)(extended, col_lists[:, :, 1:])
    own_blocks = extended[:, :, :NBLK]
    differ = own_blocks[:, :, :, None, :] - beside
    moved = jnp.einsum('nakij,nakj->naki', blocks[:, :, 1:], differ[:, OUTS], precision=lax.Precision.HIGHEST)
    term = 0.5 * jnp.einsum('ncaki,naki->nakc', differ[:, :OUTS], moved, precision=lax.Precision.HIGHEST)
    term = term.reshape(BLOCKS * 6, OUTS)
    sensitivity = jax.ops.segment_sum(term, zone_map.reshape(-1), num_segments=ZONES).T
    return (adjoint, sensitivity)
```

```python
import functools

import jax
import jax.numpy as jnp
from jax import lax
from jax.experimental import pallas as pl
from jax.experimental.pallas import tpu as pltpu
from jax.sharding import PartitionSpec as P

MESH = pl.DeviceIdType.MESH
F32 = jnp.float32
BF16 = jnp.bfloat16
NODES = 64
DOF = 64
COLS = 16
LANES = 128
GROUPS = 16
EXT = 160
ZONE_DEV = 128
PAIRS = ((0, 2), (4, 6), (1, 3), (5, None))
FACE_ROWS = 8 * COLS + 8


def nt(a, b):
    return lax.dot_general(a, b, (((1,), (1,)), ((), ())), preferred_element_type=F32)


def nn(a, b):
    return lax.dot_general(a, b, (((1,), (0,)), ((), ())), preferred_element_type=F32)


def exact_nn(a, b):
    return lax.dot_general(
        a, b, (((1,), (0,)), ((), ())), preferred_element_type=F32, precision=lax.Precision.HIGHEST
    )


def exact_nt(a, b):
    return lax.dot_general(
        a, b, (((1,), (1,)), ((), ())), preferred_element_type=F32, precision=lax.Precision.HIGHEST
    )


def halves(x):
    high = x.astype(BF16)
    return high, (x - high.astype(F32)).astype(BF16)


def thirds(x):
    high = x.astype(BF16)
    rest = x - high.astype(F32)
    mid = rest.astype(BF16)
    return high, mid, (rest - mid.astype(F32)).astype(BF16)


def iota(shape, dim):
    return lax.broadcasted_iota(jnp.int32, shape, dim)


def lower(rows=COLS):
    return iota((rows, LANES), 1) < DOF


def kernel(
    sizes,
    loads_ref, disp_ref, stiff_ref, col_ref, face_ref, zone_ref,
    adj_ref, sens_ref,
    m_ref, wh_ref, wl_ref,
    zf, zh, zl, wf, wh0, wl0,
    zp_ref, qs_ref, qp_ref, wp_ref, vp_ref, xa_ref,
    dinv_ref, dpack_ref, dsplit_ref, dext_ref, dd_ref,
    mvh_ref, mvl_ref, oh_ref, term_ref,
    zsend, wsend, zrecv, wrecv,
    g1_ref, g2_ref, g1_slots, g2_slots, x1_ref, x2_ref, x1_slots, x2_slots,
    part_ref, carry_ref,
    load_sems, z_send_sems, z_recv_sems, w_send_sems, w_recv_sems,
    red_send_sems, red_recv_sems, carry_sems,
):
    nx, ny, nz = sizes
    nb = ny * nz
    mx, my, mz = lax.axis_index("gx"), lax.axis_index("gy"), lax.axis_index("gz")
    mb = my * nz + mz
    me = mx * nb + mb
    total = nx * nb

    def along(i):
        return (lax.rem(mx + i, nx), my, mz)

    def across(i):
        b = lax.rem(mb + i, nb)
        return (mx, b // nz, lax.rem(b, nz))

    def flat(i):
        s = lax.rem(me + i + total, total)
        b = lax.rem(s, nb)
        return (s // nb, b // nz, lax.rem(b, nz))

    barrier = pltpu.get_barrier_semaphore()
    for i in range(1, nx):
        pl.semaphore_signal(barrier, inc=1, device_id=along(i), device_id_type=MESH)
    for i in range(1, nb):
        pl.semaphore_signal(barrier, inc=1, device_id=across(i), device_id_type=MESH)
    pl.semaphore_signal(barrier, inc=1, device_id=flat(-1), device_id_type=MESH)

    rows_k = NODES // 8 * 32 * 8

    def stiff_copy(k):
        part = pl.ds(k * rows_k, rows_k)
        return pltpu.make_async_copy(stiff_ref.at[part], m_ref.at[part], load_sems.at[k])

    for pair in PAIRS:
        for k in pair:
            if k is not None:
                stiff_copy(k).start()

    lo16, lo8, lo32 = lower(), lower(8), lower(32)

    prow, pcol = iota((256, 256), 0), iota((256, 256), 1)
    perm = jnp.where(
        (prow // DOF == pcol // DOF)
        & ((prow % DOF) // 32 + 2 * (prow % 32) == pcol % DOF),
        1.0, 0.0,
    ).astype(BF16)

    def put_rows(base, count, packed):
        turned = pltpu.roll(packed, DOF, 1)
        low = lower(count)
        dext_ref[pl.ds(base, count, stride=2), :] = jnp.where(low, packed, turned)
        dext_ref[pl.ds(base + 1, count, stride=2), :] = jnp.where(low, turned, packed)

    put_rows(0, 32, disp_ref[...])

    rel = lax.rem(zone_ref[...] - me * ZONE_DEV + total * ZONE_DEV, total * ZONE_DEV).astype(F32)
    rel = jnp.concatenate([jnp.zeros((1, NODES), F32), rel, jnp.zeros((1, NODES), F32)], axis=0)
    spread = jnp.where(iota((NODES, 512), 1) // 8 == iota((NODES, 512), 0), 1.0, 0.0).astype(BF16)
    spots = nn(rel.astype(BF16), spread)
    mine = iota((8, 512), 1) % 8 == iota((8, 512), 0)
    spot = jnp.sum(jnp.where(mine, spots, 0.0), axis=0, keepdims=True)
    entry = iota((1, 512), 1) % 8
    spot = jnp.where((entry == 0) | (entry == 7), -1.0, spot)
    for part in range(0, 2 * ZONE_DEV, 32):
        zone = (iota((32, 512), 0) + part).astype(F32)
        oh_ref[part : part + 32, :] = jnp.where(zone == spot, 1.0, 0.0).astype(BF16)

    stiff_copy(0).wait()
    lane8 = iota((8, LANES), 1)
    key = jnp.where(lane8 < DOF, lane8, lane8 - DOF)
    own = (key % 2 == 0) == (lane8 < DOF)
    key = jnp.where(own, key // 2, -1)

    def take_diagonal(octet, _):
        base = pl.multiple_of(octet * 256, 256)
        got = jnp.zeros((8, LANES), F32)
        for t in range(32):
            got = got + jnp.where(key == t, m_ref[pl.ds(base + t * 8, 8), :], 0.0)
        both = jnp.where(own, got, pltpu.roll(got, DOF, 1))
        dinv_ref[pl.ds(pl.multiple_of(octet * 8, 8), 8), :] = 1.0 / both
        return 0

    lax.fori_loop(0, 8, take_diagonal, 0)
    dpack_ref[...] = jnp.where(
        lo32, dinv_ref[pl.ds(0, 32, stride=2), :], dinv_ref[pl.ds(1, 32, stride=2), :]
    )
    dhi, dmid, dlo = thirds(dpack_ref[...])
    small = perm[:LANES, :LANES]
    dsplit_ref[...] = nt(dhi, small) + nt(dmid, small) + nt(dlo, small)

    def put_nodes(tile, node, full, high, low):
        turned = pltpu.roll(tile, DOF, 1)
        for i, x in enumerate((jnp.where(lo16, tile, turned), jnp.where(lo16, turned, tile))):
            full[node + i] = x
            xh, xl = halves(x)
            high[node + i] = xh
            low[node + i] = xl

    def start_z(tau, _):
        lanes = pl.ds(pl.multiple_of(tau * LANES, LANES), LANES)
        tile = loads_ref[:, lanes] * dpack_ref[pl.ds(tau, 1), :]
        zp_ref[:, lanes] = tile
        put_nodes(tile, 2 * tau, zf, zh, zl)
        return 0

    lax.fori_loop(0, 32, start_z, 0, unroll=8)

    def fill_face(d, full, buf):
        for q in range(8):
            a, b = face_ref[d, 2 * q], face_ref[d, 2 * q + 1]
            buf[d, q * COLS : (q + 1) * COLS, :] = jnp.where(lo16, full[a], full[b])

    def fill_disp(d, buf):
        got = jnp.zeros((8, LANES), F32)
        sub = iota((8, LANES), 0)
        for q in range(8):
            a, b = face_ref[d, 2 * q], face_ref[d, 2 * q + 1]
            pair = jnp.where(lower(1), dext_ref[pl.ds(a, 1), :], dext_ref[pl.ds(b, 1), :])
            got = jnp.where(sub == q, jnp.broadcast_to(pair, (8, LANES)), got)
        buf[d, 8 * COLS : FACE_ROWS, :] = got

    place = (mx, mx, my, my, mz, mz)
    counts = (nx, nx, ny, ny, nz, nz)

    def has(d):
        return place[d] > 0 if d % 2 == 0 else place[d] < counts[d] - 1

    def neighbour(d):
        step = -1 if d % 2 == 0 else 1
        there = lax.rem(place[d] + step + counts[d], counts[d])
        return ((there, my, mz), (mx, there, mz), (mx, my, there))[d // 2]

    def face_copy(d, send, recv, send_sems, recv_sems):
        return pltpu.make_async_remote_copy(
            src_ref=send.at[d], dst_ref=recv.at[d ^ 1],
            send_sem=send_sems.at[d], recv_sem=recv_sems.at[d ^ 1],
            device_id=neighbour(d), device_id_type=MESH,
        )

    def face_arrival(d, send, recv, send_sems, recv_sems):
        return pltpu.make_async_remote_copy(
            src_ref=send.at[d], dst_ref=recv.at[d],
            send_sem=send_sems.at[d], recv_sem=recv_sems.at[d],
            device_id=neighbour(d), device_id_type=MESH,
        )

    zline = (zsend, zrecv, z_send_sems, z_recv_sems)
    wline = (wsend, wrecv, w_send_sems, w_recv_sems)

    for d in range(6):
        fill_face(d, zf, zsend)
        fill_disp(d, zsend)

    pl.semaphore_wait(barrier, nx - 1 + nb - 1 + 1)

    def send_face(d, line):
        @pl.when(has(d))
        def _():
            face_copy(d, *line).start()

    def await_face(d, line):
        @pl.when(has(d))
        def _():
            face_arrival(d, *line).wait_recv()

        @pl.when(jnp.logical_not(has(d)))
        def _():
            line[1][d] = jnp.zeros(line[1].shape[1:], F32)

    def end_face(d, line):
        @pl.when(has(d))
        def _():
            face_copy(d, *line).wait_send()

    for d in range(6):
        send_face(d, zline)

    for at, (first, second) in enumerate(PAIRS):
        for k in (first, second):
            if k:
                stiff_copy(k).wait()

        def relay(octet, _, first=first, second=second, at=at):
            for s in range(8):
                base = pl.multiple_of((first * 8 + octet) * 256, 256)
                a = m_ref[pl.ds(base + s, 32, stride=8), :]
                ar = pltpu.roll(a, DOF, 1)
                if second is None:
                    b = br = jnp.zeros((32, LANES), F32)
                else:
                    base = pl.multiple_of((second * 8 + octet) * 256, 256)
                    b = m_ref[pl.ds(base + s, 32, stride=8), :]
                    br = pltpu.roll(b, DOF, 1)
                for p, x in enumerate((jnp.where(lo32, a, br), jnp.where(lo32, ar, b))):
                    xh, xl = halves(x)
                    rows = pl.ds(pl.multiple_of(octet * 512, 512) + s * DOF + p * 32, 32)
                    wh_ref[rows, at * LANES : (at + 1) * LANES] = xh
                    wl_ref[rows, at * LANES : (at + 1) * LANES] = xl
            return 0

        lax.fori_loop(0, 8, relay, 0)

    def take_face(d, line, full, high, low):
        recv = line[1]
        for q in range(8):
            put_nodes(recv[d, q * COLS : (q + 1) * COLS, :], NODES + d * 16 + 2 * q, full, high, low)

    for d in range(6):
        await_face(d, zline)
    for d in range(6):
        take_face(d, zline, zf, zh, zl)
        put_rows(NODES + d * 16, 8, zrecv[d, 8 * COLS : FACE_ROWS, :])

    def gathered(group, source, tiles, scale=None):
        rows = []
        for r4 in range(4):
            r = group * 4 + r4
            parts = []
            for at in range(tiles):
                first, second = PAIRS[at]
                a = source[col_ref[first, r]]
                b = jnp.zeros_like(a) if second is None else source[col_ref[second, r]]
                x = jnp.where(lo16, a, b)
                parts.append(x * scale if scale is not None and at == 0 else x)
            rows.append(jnp.concatenate(parts, axis=1))
        return jnp.concatenate(rows, axis=0)

    def multiply(group, high, low, tiles):
        rows = pl.ds(pl.multiple_of(group * 256, 256), 256)
        depth = tiles * LANES
        n = high.shape[0]
        weights = wh_ref[rows, :depth]
        both = nt(jnp.concatenate([high, low], axis=0), weights)
        return both[:n] + both[n:] + nt(high, wl_ref[rows, :depth])

    def own_part(x):
        return jnp.concatenate(
            [
                jnp.where(lo16, x[0:16, :LANES], x[16:32, :LANES]),
                jnp.where(lo16, x[32:48, LANES:], x[48:64, LANES:]),
            ],
            axis=1,
        )

    def image(group, _):
        out = multiply(group, gathered(group, zh, 4), gathered(group, zl, 4), 4)
        qs_ref[pl.ds(pl.multiple_of(group * COLS, COLS), COLS), :] = own_part(out)
        return 0

    lax.fori_loop(0, GROUPS, image, 0, unroll=4)

    def natural(group, _):
        rows = pl.ds(pl.multiple_of(group * 64, 64), 64)
        hi, mid, lo = thirds(qs_ref[rows, :])
        out = nn(jnp.concatenate([hi, mid, lo], axis=0), perm)
        out = out[:64] + out[64:128] + out[128:]
        for i in range(4):
            for h in range(2):
                tau = group * 8 + i * 2 + h
                lanes = pl.ds(pl.multiple_of(tau * LANES, LANES), LANES)
                tile = out[i * COLS : (i + 1) * COLS, h * LANES : (h + 1) * LANES]
                qp_ref[:, lanes] = tile
                tile = tile * dpack_ref[pl.ds(tau, 1), :]
                wp_ref[:, lanes] = tile
                put_nodes(tile, 2 * tau, wf, wh0, wl0)
        return 0

    lax.fori_loop(0, 4, natural, 0, unroll=4)

    for d in (0, 2, 4, 1, 3, 5):
        fill_face(d, wf, wsend)
        send_face(d, wline)

    def gram(left, right):
        lh, ll = halves(left)
        rh, rl = halves(right)
        both = nt(jnp.concatenate([lh, ll], axis=0), rh)
        n = left.shape[0]
        return both[:n] + both[n:] + nt(lh, rl)

    def product(step, sums):
        lanes = pl.ds(pl.multiple_of(step * 512, 512), 512)
        z, q, w = zp_ref[:, lanes], qp_ref[:, lanes], wp_ref[:, lanes]
        n0 = gram(loads_ref[:, lanes], z)
        cw = gram(jnp.concatenate([z, w], axis=0), q)
        return sums[0] + n0, sums[1] + cw[:16], sums[2] + cw[16:]

    zero16 = jnp.zeros((COLS, COLS), F32)
    grams = lax.fori_loop(0, 8, product, (zero16, zero16, zero16), unroll=4)

    row16, lane16 = iota((COLS, LANES), 0), iota((COLS, LANES), 1)
    fits16 = row16 % 8 == lane16 // 16
    sub8 = iota((8, LANES), 0)
    fits8 = sub8 == lane8 // 16

    def repeated(x):
        x = jnp.concatenate([x, jnp.zeros((COLS, LANES - COLS), F32)], axis=1)
        for by in (16, 32, 64):
            x = x + pltpu.roll(x, by, 1)
        return x

    def flattened(x):
        x = jnp.where(fits16, repeated(x), 0.0)
        return [jnp.sum(x[0:8], axis=0, keepdims=True), jnp.sum(x[8:16], axis=0, keepdims=True)]

    def unflattened(rows):
        out = []
        for row in rows:
            x = jnp.where(fits8, jnp.broadcast_to(row, (8, LANES)), 0.0)
            for by in (16, 32, 64):
                x = x + pltpu.roll(x, by, 1)
            out.append(x)
        return jnp.concatenate(out, axis=0)

    def red_copy(i, stage, src, slots, peer):
        return pltpu.make_async_remote_copy(
            src_ref=src, dst_ref=slots.at[i - 1],
            send_sem=red_send_sems.at[stage], recv_sem=red_recv_sems.at[stage],
            device_id=peer(i), device_id_type=MESH,
        )

    def red_all(stage, slots, peer):
        return pltpu.make_async_remote_copy(
            src_ref=slots, dst_ref=slots,
            send_sem=red_send_sems.at[stage], recv_sem=red_recv_sems.at[stage],
            device_id=peer(1), device_id_type=MESH,
        )

    def red_send(stage, src, slots, peer, count):
        for i in range(1, count):
            red_copy(i, stage, src, slots, peer).start()

    def red_sum(stage, src, slots, peer):
        red_all(stage, slots, peer).wait_recv()
        got = [src[...]] + [slots[i] for i in range(slots.shape[0])]
        while len(got) > 1:
            got = [a + b for a, b in zip(got[::2], got[1::2])] + got[len(got) & ~1 :]
        return got[0]

    rows = flattened(grams[0]) + flattened(grams[1]) + flattened(grams[2])
    packed = jnp.zeros((8, LANES), F32)
    for i, row in enumerate(rows):
        packed = jnp.where(sub8 == i, jnp.broadcast_to(row, (8, LANES)), packed)
    g1_ref[...] = packed
    red_send(0, g1_ref, g1_slots, along, nx)

    def differ(r, _):
        got = jnp.zeros((8, LANES), F32)
        for k in range(1, 7):
            there = jnp.broadcast_to(dext_ref[pl.ds(col_ref[k, r], 1), :], (8, LANES))
            here = jnp.broadcast_to(dext_ref[pl.ds(r, 1), :], (8, LANES))
            got = jnp.where(sub8 == k, here - there, got)
        dd_ref[pl.ds(pl.multiple_of(r * 8, 8), 8), :] = got
        return 0

    lax.fori_loop(0, NODES, differ, 0, unroll=8)

    k32, lane32 = iota((32, LANES), 0) % 8, iota((32, LANES), 1)
    fit256 = iota((32, 256), 0) // 8 == iota((32, 256), 1) // DOF

    def moved(group, _):
        rows = pl.ds(pl.multiple_of(group * 32, 32), 32)
        d = dd_ref[rows, :]
        parts = []
        for first, second in PAIRS:
            keep = (k32 == first) & (lane32 < DOF)
            if second is not None:
                keep = keep | ((k32 == second) & (lane32 >= DOF))
            parts.append(jnp.where(keep, d, 0.0))
        hi, lo = halves(jnp.concatenate(parts, axis=1))
        out = jnp.where(fit256, multiply(group, hi, lo, 4), 0.0)
        hi, lo = halves(out)
        out = nn(jnp.concatenate([hi, lo], axis=0), perm)
        mvh_ref[rows, :] = out[:32].astype(BF16)
        mvl_ref[rows, :] = out[32:].astype(BF16)
        return 0

    lax.fori_loop(0, GROUPS, moved, 0, unroll=4)

    g2_ref[...] = red_sum(0, g1_ref, g1_slots, along)
    red_send(1, g2_ref, g2_slots, across, nb)

    for d in (1, 3, 5):
        await_face(d, wline)
    for d in (1, 3, 5):
        take_face(d, wline, wf, wh0, wl0)

    half = jnp.where(lo16, 0.5, 1.0).astype(BF16)

    def curve(group, total_):
        out = multiply(group, gathered(group, wh0, 2, half), gathered(group, wl0, 2, half), 2)
        y = own_part(out)
        w = qs_ref[pl.ds(pl.multiple_of(group * COLS, COLS), COLS), :]
        w = w * jnp.concatenate(
            [dsplit_ref[pl.ds(group * 2, 1), :], dsplit_ref[pl.ds(group * 2 + 1, 1), :]], axis=1
        )
        yh, yl = halves(y)
        wh_, wl_ = halves(w)
        a = nt(jnp.concatenate([wh_, wl_], axis=0), yh)
        b = nt(jnp.concatenate([yh, yl], axis=0), wh_)
        return total_ + a[:16] + a[16:] + b[:16] + b[16:] + nt(wh_, yl) + nt(yh, wl_)

    curved = lax.fori_loop(0, GROUPS, curve, zero16, unroll=4)
    x1_ref[...] = jnp.concatenate(flattened(curved), axis=0)
    red_send(2, x1_ref, x1_slots, along, nx)

    kinds = [(iota((COLS, LANES), 1) // 32, iota((COLS, LANES), 1) % 8)]

    def terms(four, base, full):
        rows = pl.ds(pl.multiple_of(four * LANES, LANES), LANES)
        mh, ml = mvh_ref[rows, :], mvl_ref[rows, :]
        got = jnp.zeros((COLS, LANES), F32)
        for g in range(4):
            r = (four * 4 + g) * 4
            here = [jnp.where(lo16, full[r + 2 * h], full[r + 2 * h + 1]) for h in range(2)]
            parts = []
            for k in range(1, 7):
                parts.append(
                    jnp.concatenate(
                        [
                            here[h]
                            - jnp.where(
                                lo16, full[col_ref[k, r + 2 * h]], full[col_ref[k, r + 2 * h + 1]]
                            )
                            for h in range(2)
                        ],
                        axis=1,
                    )
                )
            hi, lo = halves(jnp.concatenate(parts, axis=0))
            both = nt(jnp.concatenate([hi, lo], axis=0), mh)
            out = both[:96] + both[96:] + nt(hi, ml)
            for k in range(1, 7):
                keep = (kinds[0][0] == g) & (kinds[0][1] == k)
                got = got + jnp.where(keep, out[(k - 1) * COLS : k * COLS], 0.0)
        term_ref[base : base + COLS, pl.ds(pl.multiple_of(four * LANES, LANES), LANES)] = 0.5 * got

    def terms_z(four, _):
        terms(four, 0, zf)
        return 0

    def terms_w(four, _):
        terms(four, COLS, wf)
        return 0

    lax.fori_loop(0, 4, terms_z, 0)

    x2_ref[...] = red_sum(2, x1_ref, x1_slots, along)
    red_send(3, x2_ref, x2_slots, across, nb)

    for d in (0, 2, 4):
        await_face(d, wline)
    for d in (0, 2, 4):
        take_face(d, wline, wf, wh0, wl0)
    lax.fori_loop(0, 4, terms_w, 0)

    hi, mid, lo = thirds(term_ref[...])
    sums = nt(jnp.concatenate([hi, mid, lo], axis=0), oh_ref[...])
    sums = sums[:32] + sums[32:64] + sums[64:]
    own_sums = sums[:, :ZONE_DEV]
    part_ref[...] = sums[:, ZONE_DEV:]
    carry = pltpu.make_async_remote_copy(
        src_ref=part_ref, dst_ref=carry_ref, send_sem=carry_sems.at[0], recv_sem=carry_sems.at[1],
        device_id=flat(1), device_id_type=MESH,
    )
    carry.start()

    def solved(x):
        n = x.shape[0]
        lane = iota((1, LANES), 1) % COLS
        for k in range(COLS):
            inv = 1.0 / x[k : k + 1, k : k + 1]
            column = jnp.broadcast_to(x[:, k : k + 1], (n, LANES)) * inv
            x = jnp.where(lane == k, column, x - column * jnp.broadcast_to(x[k : k + 1, :], (n, LANES)))
        return x[COLS:]

    g = red_sum(1, g2_ref, g2_slots, across)
    n0 = unflattened([g[0:1], g[1:2]])
    c0 = unflattened([g[2:3], g[3:4]])
    w0 = unflattened([g[4:5], g[5:6]])
    first = solved(jnp.concatenate([c0, n0, w0], axis=0))
    step0, mix = first[:COLS], first[COLS:]
    low16 = lane16 < COLS
    step0_, mix_ = jnp.where(low16, step0, 0.0), jnp.where(low16, mix, 0.0)

    pad = jnp.zeros((LANES - COLS, LANES), F32)

    def times(a, b):
        return exact_nn(a, jnp.concatenate([b, pad], axis=0))

    mix_w = times(mix_, w0)
    right = times(step0_, w0) - c0

    both = jnp.concatenate([step0[:, :COLS], mix[:, :COLS]], axis=0)
    bh, bm, bl = thirds(both)
    lhs = jnp.concatenate([bh, bh, bm, bh, bm, bl], axis=1)

    def prepare(step, _):
        lanes = pl.ds(pl.multiple_of(step * 512, 512), 512)
        ah, am, al = thirds(zp_ref[:, lanes])
        out = nn(lhs, jnp.concatenate([ah, am, ah, al, am, ah], axis=0))
        xa_ref[:, lanes] = out[:16]
        ah, am, al = thirds(out[16:] - wp_ref[:, lanes])
        vp_ref[0:16, lanes] = ah
        vp_ref[16:32, lanes] = am
        vp_ref[32:48, lanes] = al
        return 0

    lax.fori_loop(0, 8, prepare, 0, unroll=2)

    carry.wait_recv()
    all_sums = own_sums + carry_ref[...]
    ah, am, al = thirds(all_sums[:16])
    out = nn(lhs, jnp.concatenate([ah, am, ah, al, am, ah], axis=0))
    sens_a = out[:16]
    sens_v = thirds(out[16:] - all_sums[16:])

    x = red_sum(3, x2_ref, x2_slots, across)
    x = unflattened([x[0:1], x[1:2]])
    y = solved(jnp.concatenate([x - mix_w, right], axis=0))[:, :COLS]
    yh, ym, yl = thirds(y)
    lhs = jnp.concatenate([yh, yh, ym, yh, ym, yl], axis=1)

    def finish(step, _):
        lanes = pl.ds(pl.multiple_of(step * 512, 512), 512)
        v = vp_ref[:, lanes]
        ah, am, al = v[0:16], v[16:32], v[32:48]
        out = nn(lhs, jnp.concatenate([ah, am, ah, al, am, ah], axis=0))
        adj_ref[:, lanes] = xa_ref[:, lanes] + out
        return 0

    lax.fori_loop(0, 8, finish, 0, unroll=4)
    ah, am, al = sens_v
    sens_ref[...] = sens_a + nn(lhs, jnp.concatenate([ah, am, ah, al, am, ah], axis=0))

    for d in range(6):
        end_face(d, zline)
        end_face(d, wline)
    red_all(0, g1_slots, along).wait_send()
    red_all(1, g2_slots, across).wait_send()
    red_all(2, x1_slots, along).wait_send()
    red_all(3, x2_slots, across).wait_send()
    carry.wait_send()


def on_device(sizes, loads, displacement, stiffness, col_index, face_index, zone_map):
    nx, ny, nz = sizes
    nb = ny * nz
    tiles = jnp.transpose(stiffness, (1, 0, 2)).reshape(7, 8, 8, 32, LANES)
    tiles = jnp.transpose(tiles, (0, 1, 3, 2, 4)).reshape(7 * 8 * 32 * 8, LANES)
    vmem = pl.BlockSpec(memory_space=pltpu.VMEM)
    smem = pl.BlockSpec(memory_space=pltpu.SMEM)
    dma = pltpu.SemaphoreType.DMA
    v = pltpu.VMEM
    return pl.pallas_call(
        functools.partial(kernel, sizes),
        out_shape=(
            jax.ShapeDtypeStruct((COLS, NODES * DOF), F32),
            jax.ShapeDtypeStruct((COLS, ZONE_DEV), F32),
        ),
        in_specs=[vmem, vmem, pl.BlockSpec(memory_space=pl.ANY), smem, smem, vmem],
        out_specs=(vmem, vmem),
        scratch_shapes=[
            v((7 * 8 * 32 * 8, LANES), F32),
            v((NODES * DOF, 512), BF16), v((NODES * DOF, 512), BF16),
            v((EXT, COLS, LANES), F32), v((EXT, COLS, LANES), BF16), v((EXT, COLS, LANES), BF16),
            v((EXT, COLS, LANES), F32), v((EXT, COLS, LANES), BF16), v((EXT, COLS, LANES), BF16),
            v((COLS, NODES * DOF), F32), v((GROUPS * COLS, 256), F32),
            v((COLS, NODES * DOF), F32), v((COLS, NODES * DOF), F32),
            v((3 * COLS, NODES * DOF), BF16), v((COLS, NODES * DOF), F32),
            v((NODES, LANES), F32), v((32, LANES), F32), v((32, LANES), F32),
            v((EXT, LANES), F32), v((NODES * 8, LANES), F32),
            v((NODES * 8, 256), BF16), v((NODES * 8, 256), BF16),
            v((2 * ZONE_DEV, 512), BF16), v((2 * COLS, 512), F32),
            v((6, FACE_ROWS, LANES), F32), v((6, 8 * COLS, LANES), F32),
            v((6, FACE_ROWS, LANES), F32), v((6, 8 * COLS, LANES), F32),
            v((8, LANES), F32), v((8, LANES), F32),
            v((nx - 1, 8, LANES), F32), v((nb - 1, 8, LANES), F32),
            v((2, LANES), F32), v((2, LANES), F32),
            v((nx - 1, 2, LANES), F32), v((nb - 1, 2, LANES), F32),
            v((2 * COLS, ZONE_DEV), F32), v((2 * COLS, ZONE_DEV), F32),
            dma((7,)), dma((6,)), dma((6,)), dma((6,)), dma((6,)),
            dma((4,)), dma((4,)), dma((2,)),
        ],
        compiler_params=pltpu.CompilerParams(
            collective_id=0, has_side_effects=True, vmem_limit_bytes=48 * 1024 * 1024
        ),
        cost_estimate=pl.CostEstimate(
            flops=400_000_000, bytes_accessed=8_000_000, transcendentals=0
        ),
    )(
        loads, displacement.reshape(32, LANES), tiles,
        jnp.transpose(col_index), face_index, jnp.transpose(zone_map),
    )


def solution(mesh):
    sizes = (mesh.shape["gx"], mesh.shape["gy"], mesh.shape["gz"])
    axes = ("gx", "gy", "gz")
    in_specs = (
        P(None, axes), P(axes), P(axes, None, None), P(axes, None), P(axes, None), P(axes, None),
    )
    return jax.shard_map(
        functools.partial(on_device, sizes), mesh=mesh, in_specs=in_specs,
        out_specs=(P(None, axes), P(None, axes)), check_vma=False,
    )
```

```python
import functools

import jax
import jax.numpy as jnp
from jax import lax
from jax.experimental import pallas as pl
from jax.experimental.pallas import tpu as pltpu
from jax.sharding import PartitionSpec as P

MESH = pl.DeviceIdType.MESH
F32 = jnp.float32
BF16 = jnp.bfloat16
NODES = 64
DOF = 64
COLS = 16
LANES = 128
GROUPS = 16
EXT = 160
ZONE_DEV = 128
PAIRS = ((0, 2), (4, 6), (1, 3), (5, None))
FACE_ROWS = 8 * COLS + 8


def nt(a, b):
    return lax.dot_general(a, b, (((1,), (1,)), ((), ())), preferred_element_type=F32)


def nn(a, b):
    return lax.dot_general(a, b, (((1,), (0,)), ((), ())), preferred_element_type=F32)


def exact_nn(a, b):
    return lax.dot_general(
        a, b, (((1,), (0,)), ((), ())), preferred_element_type=F32, precision=lax.Precision.HIGHEST
    )


def exact_nt(a, b):
    return lax.dot_general(
        a, b, (((1,), (1,)), ((), ())), preferred_element_type=F32, precision=lax.Precision.HIGHEST
    )


def halves(x):
    high = x.astype(BF16)
    return high, (x - high.astype(F32)).astype(BF16)


def thirds(x):
    high = x.astype(BF16)
    rest = x - high.astype(F32)
    mid = rest.astype(BF16)
    return high, mid, (rest - mid.astype(F32)).astype(BF16)


def iota(shape, dim):
    return lax.broadcasted_iota(jnp.int32, shape, dim)


def lower(rows=COLS):
    return iota((rows, LANES), 1) < DOF


def kernel(
    sizes,
    loads_in, disp_in, stiff_ref, col_in, face_in, zone_in,
    adj_ref, sens_ref,
    loads_ref, disp_ref, col_ref, face_ref, zone_ref,
    m_ref, w_ref,
    zf, zh, zl, wf, wh0, wl0,
    zp_ref, qs_ref, qp_ref, wp_ref, vp_ref, xa_ref,
    dinv_ref, dpack_ref, dsplit_ref, dext_ref, dd_ref,
    mm_ref, mv_ref, pushed_ref, out_ref, oh_ref, term_ref, perm_ref,
    zsend, wsend, zrecv, wrecv,
    g1_ref, g2_ref, g1_slots, g2_slots, x1_ref, x2_ref, x1_slots, x2_slots,
    part_ref, carry_ref,
    load_sems, input_sems, z_send_sems, z_recv_sems, w_send_sems, w_recv_sems,
    red_send_sems, red_recv_sems, carry_sems,
):
    nx, ny, nz = sizes
    nb = ny * nz
    mx, my, mz = lax.axis_index("gx"), lax.axis_index("gy"), lax.axis_index("gz")
    mb = my * nz + mz
    me = mx * nb + mb
    total = nx * nb

    def along(i):
        return (lax.rem(mx + i, nx), my, mz)

    def across(i):
        b = lax.rem(mb + i, nb)
        return (mx, b // nz, lax.rem(b, nz))

    def flat(i):
        s = lax.rem(me + i + total, total)
        b = lax.rem(s, nb)
        return (s // nb, b // nz, lax.rem(b, nz))

    barrier = pltpu.get_barrier_semaphore()
    for i in range(1, nx):
        pl.semaphore_signal(barrier, inc=1, device_id=along(i), device_id_type=MESH)
    for i in range(1, nb):
        pl.semaphore_signal(barrier, inc=1, device_id=across(i), device_id_type=MESH)
    pl.semaphore_signal(barrier, inc=1, device_id=flat(-1), device_id_type=MESH)

    rows_k = NODES // 8 * 32 * 8

    def stiff_copy(k):
        part = pl.ds(k * rows_k, rows_k)
        return pltpu.make_async_copy(stiff_ref.at[part], m_ref.at[part], load_sems.at[k])

    inputs = [
        pltpu.make_async_copy(a, b, input_sems.at[i])
        for i, (a, b) in enumerate((
            (loads_in, loads_ref), (disp_in, disp_ref), (face_in, face_ref), (zone_in, zone_ref),
            (col_in, col_ref),
        ))
    ]
    stiff_copy(0).start()
    for copy in inputs:
        copy.start()
    for pair in PAIRS:
        for k in pair:
            if k:
                stiff_copy(k).start()

    lo16, lo8, lo32 = lower(), lower(8), lower(32)

    prow, pcol = iota((256, 256), 0), iota((256, 256), 1)
    perm_ref[...] = jnp.where(
        (prow // DOF == pcol // DOF)
        & ((prow % DOF) // 32 + 2 * (prow % 32) == pcol % DOF),
        1.0, 0.0,
    ).astype(BF16)

    wh0[NODES:] = jnp.zeros((EXT - NODES, COLS, LANES), BF16)
    wl0[NODES:] = jnp.zeros((EXT - NODES, COLS, LANES), BF16)

    def put_rows(base, count, packed):
        turned = pltpu.roll(packed, DOF, 1)
        low = lower(count)
        dext_ref[pl.ds(base, count, stride=2), :] = jnp.where(low, packed, turned)
        dext_ref[pl.ds(base + 1, count, stride=2), :] = jnp.where(low, turned, packed)

    inputs[1].wait()
    put_rows(0, 32, disp_ref[...])

    inputs[3].wait()
    rel = lax.rem(zone_ref[...] - me * ZONE_DEV + total * ZONE_DEV, total * ZONE_DEV).astype(F32)
    rel = jnp.concatenate([jnp.zeros((1, NODES), F32), rel, jnp.zeros((1, NODES), F32)], axis=0)
    spread = jnp.where(iota((NODES, 512), 1) // 8 == iota((NODES, 512), 0), 1.0, 0.0).astype(BF16)
    spots = nn(rel.astype(BF16), spread)
    mine = iota((8, 512), 1) % 8 == iota((8, 512), 0)
    spot = jnp.sum(jnp.where(mine, spots, 0.0), axis=0, keepdims=True)
    entry = iota((1, 512), 1) % 8
    spot = jnp.where((entry == 0) | (entry == 7), -1.0, spot)
    for part in range(0, 2 * ZONE_DEV, 32):
        zone = (iota((32, 512), 0) + part).astype(F32)
        oh_ref[part : part + 32, :] = jnp.where(zone == spot, 1.0, 0.0).astype(BF16)

    stiff_copy(0).wait()
    lane8 = iota((8, LANES), 1)
    key = jnp.where(lane8 < DOF, lane8, lane8 - DOF)
    own = (key % 2 == 0) == (lane8 < DOF)
    key = jnp.where(own, key // 2, -1)

    def take_diagonal(quarter, _):
        got = [jnp.zeros((8, LANES), F32)] * 4
        for t in range(32):
            hit = key == t
            for i in range(4):
                base = pl.multiple_of(quarter * 1024, 1024)
                got[i] = jnp.where(hit, m_ref[pl.ds(base + i * 256 + t * 8, 8), :], got[i])
        for i in range(4):
            both = jnp.where(own, got[i], pltpu.roll(got[i], DOF, 1))
            rows = pl.ds(pl.multiple_of(quarter * 32, 32) + i * 8, 8)
            dinv_ref[rows, :] = 1.0 / both
        return 0

    lax.fori_loop(0, 2, take_diagonal, 0)
    dpack_ref[...] = jnp.where(
        lo32, dinv_ref[pl.ds(0, 32, stride=2), :], dinv_ref[pl.ds(1, 32, stride=2), :]
    )
    dhi, dmid, dlo = thirds(dpack_ref[...])
    small = perm_ref[:LANES, :LANES]
    dsplit_ref[...] = nt(dhi, small) + nt(dmid, small) + nt(dlo, small)

    def put_nodes(tile, node, full, high, low):
        turned = pltpu.roll(tile, DOF, 1)
        for i, x in enumerate((jnp.where(lo16, tile, turned), jnp.where(lo16, turned, tile))):
            full[node + i] = x
            xh, xl = halves(x)
            high[node + i] = xh
            low[node + i] = xl

    def put_full(tile, node, full):
        turned = pltpu.roll(tile, DOF, 1)
        full[node] = jnp.where(lo16, tile, turned)
        full[node + 1] = jnp.where(lo16, turned, tile)

    def start_z(tau, _):
        lanes = pl.ds(pl.multiple_of(tau * LANES, LANES), LANES)
        tile = loads_ref[:, lanes] * dpack_ref[pl.ds(tau, 1), :]
        zp_ref[:, lanes] = tile
        put_nodes(tile, 2 * tau, zf, zh, zl)
        return 0

    inputs[0].wait()
    lax.fori_loop(0, 32, start_z, 0, unroll=32)

    def fill_face(d, full, buf):
        for q in range(8):
            a, b = face_ref[d, 2 * q], face_ref[d, 2 * q + 1]
            buf[d, q * COLS : (q + 1) * COLS, :] = jnp.where(lo16, full[a], full[b])

    def fill_disp(d, buf):
        got = jnp.zeros((8, LANES), F32)
        sub = iota((8, LANES), 0)
        for q in range(8):
            a, b = face_ref[d, 2 * q], face_ref[d, 2 * q + 1]
            pair = jnp.where(lower(1), dext_ref[pl.ds(a, 1), :], dext_ref[pl.ds(b, 1), :])
            got = jnp.where(sub == q, jnp.broadcast_to(pair, (8, LANES)), got)
        buf[d, 8 * COLS : FACE_ROWS, :] = got

    place = (mx, mx, my, my, mz, mz)
    counts = (nx, nx, ny, ny, nz, nz)

    def has(d):
        return place[d] > 0 if d % 2 == 0 else place[d] < counts[d] - 1

    def neighbour(d):
        step = -1 if d % 2 == 0 else 1
        there = lax.rem(place[d] + step + counts[d], counts[d])
        return ((there, my, mz), (mx, there, mz), (mx, my, there))[d // 2]

    def face_copy(d, send, recv, send_sems, recv_sems):
        return pltpu.make_async_remote_copy(
            src_ref=send.at[d], dst_ref=recv.at[d ^ 1],
            send_sem=send_sems.at[d], recv_sem=recv_sems.at[d ^ 1],
            device_id=neighbour(d), device_id_type=MESH,
        )

    def face_arrival(d, send, recv, send_sems, recv_sems):
        return pltpu.make_async_remote_copy(
            src_ref=send.at[d], dst_ref=recv.at[d],
            send_sem=send_sems.at[d], recv_sem=recv_sems.at[d],
            device_id=neighbour(d), device_id_type=MESH,
        )

    zline = (zsend, zrecv, z_send_sems, z_recv_sems)
    wline = (wsend, wrecv, w_send_sems, w_recv_sems)

    inputs[2].wait()
    for d in range(6):
        fill_face(d, zf, zsend)
        fill_disp(d, zsend)

    pl.semaphore_wait(barrier, nx - 1 + nb - 1 + 1)

    def send_face(d, line):
        @pl.when(has(d))
        def _():
            face_copy(d, *line).start()

    def await_face(d, line):
        @pl.when(has(d))
        def _():
            face_arrival(d, *line).wait_recv()

        @pl.when(jnp.logical_not(has(d)))
        def _():
            line[1][d] = jnp.zeros(line[1].shape[1:], F32)

    def end_face(d, line):
        @pl.when(has(d))
        def _():
            face_copy(d, *line).wait_send()

    for d in range(6):
        send_face(d, zline)

    for at, (first, second) in enumerate(PAIRS):
        for k in (first, second):
            if k:
                stiff_copy(k).wait()

        def relay(octet, _, first=first, second=second, at=at):
            for s in range(8):
                base = pl.multiple_of((first * 8 + octet) * 256, 256)
                a = m_ref[pl.ds(base + s, 32, stride=8), :]
                if second is None:
                    b = jnp.zeros((32, LANES), F32)
                else:
                    base = pl.multiple_of((second * 8 + octet) * 256, 256)
                    b = m_ref[pl.ds(base + s, 32, stride=8), :]
                turned = pltpu.roll(jnp.where(lo32, b, a), DOF, 1)
                for p, x in enumerate((jnp.where(lo32, a, turned), jnp.where(lo32, turned, b))):
                    xh, xl = halves(x)
                    row = pl.multiple_of(octet * 1024, 1024) + (s // 4) * 512 + (s % 4) * DOF + p * 32
                    w_ref[pl.ds(row, 32), at * LANES : (at + 1) * LANES] = xh
                    w_ref[pl.ds(row + 256, 32), at * LANES : (at + 1) * LANES] = xl
            return 0

        lax.fori_loop(0, 8, relay, 0, unroll=8)

    def take_face(d, line, full, high, low):
        recv = line[1]
        for q in range(8):
            put_nodes(recv[d, q * COLS : (q + 1) * COLS, :], NODES + d * 16 + 2 * q, full, high, low)

    inputs[4].wait()
    for d in range(6):
        await_face(d, zline)
    for d in range(6):
        take_face(d, zline, zf, zh, zl)
        put_rows(NODES + d * 16, 8, zrecv[d, 8 * COLS : FACE_ROWS, :])

    def gathered(group, source):
        rows = []
        for r4 in range(4):
            r = group * 4 + r4
            parts = []
            for first, second in PAIRS:
                a = source[col_ref[first, r]]
                b = jnp.zeros_like(a) if second is None else source[col_ref[second, r]]
                parts.append(jnp.where(lo16, a, b))
            rows.append(jnp.concatenate(parts, axis=1))
        return jnp.concatenate(rows, axis=0)

    def own_part(x):
        return jnp.concatenate(
            [
                jnp.where(lo16, x[0:16, :LANES], x[16:32, :LANES]),
                jnp.where(lo16, x[32:48, LANES:], x[48:64, LANES:]),
            ],
            axis=1,
        )

    sub8 = iota((8, LANES), 0)
    def differ(r, _):
        got = jnp.zeros((8, LANES), F32)
        for k in range(1, 7):
            there = jnp.broadcast_to(dext_ref[pl.ds(col_ref[k, r], 1), :], (8, LANES))
            here = jnp.broadcast_to(dext_ref[pl.ds(r, 1), :], (8, LANES))
            got = jnp.where(sub8 == k, here - there, got)
        dd_ref[pl.ds(pl.multiple_of(r * 8, 8), 8), :] = got
        return 0

    lax.fori_loop(0, NODES, differ, 0, unroll=16)

    k32, lane32 = iota((32, LANES), 0) % 8, iota((32, LANES), 1)
    fit256 = iota((32, 256), 0) // 8 == iota((32, 256), 1) // DOF

    def image(group, _):
        small = pl.ds(pl.multiple_of(group * 32, 32), 32)
        d = dd_ref[small, :]
        parts = []
        for first, second in PAIRS:
            keep = (k32 == first) & (lane32 < DOF)
            if second is not None:
                keep = keep | ((k32 == second) & (lane32 >= DOF))
            parts.append(jnp.where(keep, d, 0.0))
        hi, lo = halves(jnp.concatenate(parts, axis=1))
        rows = pl.ds(pl.multiple_of(group * 512, 512), 512)
        left = jnp.concatenate([gathered(group, zh), hi, gathered(group, zl), lo], axis=0)
        out = nt(left, w_ref[rows, :])
        out = out[:96, :256] + (out[96:, :256] + (out[:96, 256:] + out[96:, 256:]))
        qs_ref[pl.ds(pl.multiple_of(group * COLS, COLS), COLS), :] = own_part(out)
        hi, lo = halves(jnp.where(fit256, out[64:96], 0.0))
        row = pl.multiple_of((group // 2) * 128, 128) + (group % 2) * 32
        mm_ref[pl.ds(pl.multiple_of(row, 32), 32), :] = hi
        mm_ref[pl.ds(pl.multiple_of(row + 64, 32), 32), :] = lo
        return 0

    lax.fori_loop(0, GROUPS, image, 0, unroll=16)

    def natural(group, _):
        rows = pl.ds(pl.multiple_of(group * 64, 64), 64)
        hi, mid, lo = thirds(qs_ref[rows, :])
        out = nn(jnp.concatenate([hi, mid, lo], axis=0), perm_ref[...])
        out = out[:64] + out[64:128] + out[128:]
        for i in range(4):
            for h in range(2):
                tau = group * 8 + i * 2 + h
                lanes = pl.ds(pl.multiple_of(tau * LANES, LANES), LANES)
                tile = out[i * COLS : (i + 1) * COLS, h * LANES : (h + 1) * LANES]
                qp_ref[:, lanes] = tile
                tile = tile * dpack_ref[pl.ds(tau, 1), :]
                wp_ref[:, lanes] = tile
                put_nodes(tile, 2 * tau, wf, wh0, wl0)
        return 0

    lax.fori_loop(0, 4, natural, 0, unroll=4)

    for d in (0, 2, 4, 1, 3, 5):
        fill_face(d, wf, wsend)
        send_face(d, wline)

    def split_w(group, _):
        rows = pl.ds(pl.multiple_of(group * COLS, COLS), COLS)
        by = [dsplit_ref[pl.ds(group * 2 + h, 1), :] for h in range(2)]
        qs_ref[rows, :] = qs_ref[rows, :] * jnp.concatenate(by, axis=1)
        return 0

    lax.fori_loop(0, GROUPS, split_w, 0, unroll=4)

    def gram(left, right):
        n, m = left.shape[0], right.shape[0]
        out = nt(jnp.concatenate(halves(left), axis=0), jnp.concatenate(halves(right), axis=0))
        return out[:n, :m] + (out[n:, :m] + (out[:n, m:] + out[n:, m:]))

    def product(step, sums):
        lanes = pl.ds(pl.multiple_of(step * 512, 512), 512)
        z, q, w = zp_ref[:, lanes], qp_ref[:, lanes], wp_ref[:, lanes]
        n0 = gram(loads_ref[:, lanes], z)
        cw = gram(jnp.concatenate([z, w], axis=0), q)
        return sums[0] + n0, sums[1] + cw[:16], sums[2] + cw[16:]

    zero16 = jnp.zeros((COLS, COLS), F32)
    grams = lax.fori_loop(0, 8, product, (zero16, zero16, zero16), unroll=8)

    row16, lane16 = iota((COLS, LANES), 0), iota((COLS, LANES), 1)
    fits16 = row16 % 8 == lane16 // 16
    fits8 = sub8 == lane8 // 16

    def repeated(x):
        x = jnp.concatenate([x, jnp.zeros((COLS, LANES - COLS), F32)], axis=1)
        for by in (16, 32, 64):
            x = x + pltpu.roll(x, by, 1)
        return x

    def flattened(x):
        x = jnp.where(fits16, repeated(x), 0.0)
        return [jnp.sum(x[0:8], axis=0, keepdims=True), jnp.sum(x[8:16], axis=0, keepdims=True)]

    def unflattened(rows):
        out = []
        for row in rows:
            x = jnp.where(fits8, jnp.broadcast_to(row, (8, LANES)), 0.0)
            for by in (16, 32, 64):
                x = x + pltpu.roll(x, by, 1)
            out.append(x)
        return jnp.concatenate(out, axis=0)

    def red_copy(i, stage, src, slots, peer):
        return pltpu.make_async_remote_copy(
            src_ref=src, dst_ref=slots.at[i - 1],
            send_sem=red_send_sems.at[stage], recv_sem=red_recv_sems.at[stage],
            device_id=peer(i), device_id_type=MESH,
        )

    def red_all(stage, slots, peer):
        return pltpu.make_async_remote_copy(
            src_ref=slots, dst_ref=slots,
            send_sem=red_send_sems.at[stage], recv_sem=red_recv_sems.at[stage],
            device_id=peer(1), device_id_type=MESH,
        )

    def red_send(stage, src, slots, peer, count):
        for i in range(1, count):
            red_copy(i, stage, src, slots, peer).start()

    def red_sum(stage, src, slots, peer):
        red_all(stage, slots, peer).wait_recv()
        got = [src[...]] + [slots[i] for i in range(slots.shape[0])]
        while len(got) > 1:
            got = [a + b for a, b in zip(got[::2], got[1::2])] + got[len(got) & ~1 :]
        return got[0]

    rows = flattened(grams[0]) + flattened(grams[1]) + flattened(grams[2])
    packed = jnp.zeros((8, LANES), F32)
    for i, row in enumerate(rows):
        packed = jnp.where(sub8 == i, jnp.broadcast_to(row, (8, LANES)), packed)
    g1_ref[...] = packed
    red_send(0, g1_ref, g1_slots, along, nx)

    half = jnp.where(lo16, 0.5, 1.0)
    block256 = iota((COLS, 256), 1) // DOF

    def push(group, _):
        w = qs_ref[pl.ds(pl.multiple_of(group * COLS, COLS), COLS), :]
        left = jnp.concatenate([jnp.where(block256 == i, w, 0.0) for i in range(4)], axis=0)
        base = pl.multiple_of(group * 512, 512)
        left = jnp.concatenate(halves(left), axis=0)
        a = nn(left, w_ref[pl.ds(base, 256), :256])
        b = nn(left, w_ref[pl.ds(pl.multiple_of(base + 256, 256), 256), :256])
        out = a[:64] + (a[64:] + (b[:64] + b[64:]))
        for i in range(4):
            rows = out[i * COLS : (i + 1) * COLS]
            pushed_ref[group * 4 + i, :, :LANES] = rows[:, :LANES] * half
            pushed_ref[group * 4 + i, :, LANES:] = rows[:, LANES:]
        return 0

    lax.fori_loop(0, GROUPS, push, 0, unroll=8)

    g2_ref[...] = red_sum(0, g1_ref, g1_slots, along)
    red_send(1, g2_ref, g2_slots, across, nb)

    def within(step, total_):
        left, high, low = [], [], []
        for i in range(4):
            r = step * 4 + i
            left.append(pushed_ref[r])
            for first, second in PAIRS[:2]:
                a, b = col_ref[first, r], col_ref[second, r]
                high.append(jnp.where(lo16, wh0[a], wh0[b]))
                low.append(jnp.where(lo16, wl0[a], wl0[b]))
        left = jnp.concatenate(halves(jnp.concatenate(left, axis=1)), axis=0)
        right = jnp.concatenate([jnp.concatenate(high, axis=1), jnp.concatenate(low, axis=1)], axis=0)
        out = nt(left, right)
        return total_ + out[:16, :16] + (out[16:, :16] + (out[:16, 16:] + out[16:, 16:]))

    inside = lax.fori_loop(0, GROUPS, within, zero16, unroll=16)
    unit = jnp.where(iota((COLS, COLS), 0) == iota((COLS, COLS), 1), 1.0, 0.0)
    inside = inside + exact_nt(unit, inside)

    for at, (d, tile, upper) in enumerate(((1, 0, True), (3, 1, False), (5, 1, True))):
        for q in range(8):
            a = pushed_ref[face_ref[d, 2 * q], :, tile * LANES : (tile + 1) * LANES]
            b = pushed_ref[face_ref[d, 2 * q + 1], :, tile * LANES : (tile + 1) * LANES]
            x = jnp.where(lo16, pltpu.roll(a, DOF, 1), b) if upper else jnp.where(lo16, a, pltpu.roll(b, DOF, 1))
            out_ref[:, (at * 8 + q) * LANES : (at * 8 + q + 1) * LANES] = x

    for d in (1, 3, 5):
        await_face(d, wline)
    curved = inside
    for at, d in enumerate((1, 3, 5)):
        there = jnp.concatenate([wrecv[d, q * COLS : (q + 1) * COLS, :] for q in range(8)], axis=1)
        here = out_ref[:, at * 1024 : (at + 1) * 1024]
        curved = curved + (gram(here, there) + gram(there, here))
    x1_ref[...] = jnp.concatenate(flattened(curved), axis=0)
    red_send(2, x1_ref, x1_slots, along, nx)

    def moved_natural(four, _):
        rows = pl.ds(pl.multiple_of(four * 256, 256), 256)
        mv_ref[rows, :] = nn(mm_ref[rows, :], perm_ref[...]).astype(BF16)
        return 0

    lax.fori_loop(0, 4, moved_natural, 0, unroll=4)

    pair_at, kind = iota((COLS, LANES), 1) // 32 % 2, iota((COLS, LANES), 1) % 8

    def terms(four, base, full):
        pairs = []
        for pair in range(2):
            weights = mv_ref[pl.ds(pl.multiple_of(four * 256, 256) + pair * 128, 128), :]
            got = jnp.zeros((COLS, LANES), F32)
            for g in range(2):
                r = (four * 4 + pair * 2 + g) * 4
                here = [jnp.where(lo16, full[r + 2 * h], full[r + 2 * h + 1]) for h in range(2)]
                parts = []
                for k in range(1, 7):
                    there = [
                        jnp.where(lo16, full[col_ref[k, r + 2 * h]], full[col_ref[k, r + 2 * h + 1]])
                        for h in range(2)
                    ]
                    parts.append(jnp.concatenate([here[h] - there[h] for h in range(2)], axis=1))
                hi, lo = halves(jnp.concatenate(parts, axis=0))
                out = nt(jnp.concatenate([hi, lo], axis=0), weights)
                out = out[:96] + out[96:]
                for k in range(1, 7):
                    keep = (pair_at == g) & (kind == k)
                    got = jnp.where(keep, out[(k - 1) * COLS : k * COLS], got)
            pairs.append(got + pltpu.roll(got, DOF, 1))
        lanes = pl.ds(pl.multiple_of(four * LANES, LANES), LANES)
        term_ref[base : base + COLS, lanes] = 0.5 * jnp.where(lo16, pairs[0], pairs[1])

    def terms_z(four, _):
        terms(four, 0, zf)
        return 0

    def terms_w(four, _):
        terms(four, COLS, wf)
        return 0

    def solved(x, panel=4):
        n = x.shape[0]
        lane = iota((1, LANES), 1) % COLS
        for first in range(0, COLS, panel):
            cols = [
                jnp.broadcast_to(x[:, k : k + 1], (n, LANES)) for k in range(first, first + panel)
            ]
            for j in range(panel):
                k = first + j
                scaled = cols[j] * (1.0 / cols[j][k : k + 1, :])
                cols = [
                    scaled if i == j else c - scaled * c[k : k + 1, :] for i, c in enumerate(cols)
                ]
            new = x
            for j in range(panel):
                new = new - cols[j] * x[first + j : first + j + 1, :]
            for j in range(panel):
                new = jnp.where(lane == first + j, cols[j], new)
            x = new
        return x[COLS:]

    g = red_sum(1, g2_ref, g2_slots, across)
    n0 = unflattened([g[0:1], g[1:2]])
    c0 = unflattened([g[2:3], g[3:4]])
    w0 = unflattened([g[4:5], g[5:6]])
    first = solved(jnp.concatenate([c0, n0, w0], axis=0))
    step0, mix = first[:COLS], first[COLS:]
    low16 = lane16 < COLS
    step0_, mix_ = jnp.where(low16, step0, 0.0), jnp.where(low16, mix, 0.0)

    pad = jnp.zeros((LANES - COLS, LANES), F32)

    def times(a, b):
        return exact_nn(a, jnp.concatenate([b, pad], axis=0))

    mix_w = times(mix_, w0)
    right = times(step0_, w0) - c0

    both = jnp.concatenate([step0[:, :COLS], mix[:, :COLS]], axis=0)
    bh, bm, bl = thirds(both)
    lhs = jnp.concatenate([bh, bh, bm, bh, bm, bl], axis=1)

    def prepare(step, _):
        lanes = pl.ds(pl.multiple_of(step * 512, 512), 512)
        ah, am, al = thirds(zp_ref[:, lanes])
        out = nn(lhs, jnp.concatenate([ah, am, ah, al, am, ah], axis=0))
        xa_ref[:, lanes] = out[:16]
        ah, am, al = thirds(out[16:] - wp_ref[:, lanes])
        vp_ref[0:16, lanes] = ah
        vp_ref[16:32, lanes] = am
        vp_ref[32:48, lanes] = al
        return 0

    lax.fori_loop(0, 8, prepare, 0, unroll=8)

    x2_ref[...] = red_sum(2, x1_ref, x1_slots, along)
    red_send(3, x2_ref, x2_slots, across, nb)

    lax.fori_loop(0, 4, terms_z, 0, unroll=4)


    for d in (0, 2, 4):
        await_face(d, wline)
    for d in range(6):
        for q in range(8):
            put_full(wrecv[d, q * COLS : (q + 1) * COLS, :], NODES + d * 16 + 2 * q, wf)
    lax.fori_loop(0, 4, terms_w, 0, unroll=4)

    hi, mid, lo = thirds(term_ref[...])
    sums = nt(jnp.concatenate([hi, mid, lo], axis=0), oh_ref[...])
    sums = sums[:32] + sums[32:64] + sums[64:]
    own_sums = sums[:, :ZONE_DEV]
    part_ref[...] = sums[:, ZONE_DEV:]
    carry = pltpu.make_async_remote_copy(
        src_ref=part_ref, dst_ref=carry_ref, send_sem=carry_sems.at[0], recv_sem=carry_sems.at[1],
        device_id=flat(1), device_id_type=MESH,
    )
    carry.start()

    carry.wait_recv()
    all_sums = own_sums + carry_ref[...]
    ah, am, al = thirds(all_sums[:16])
    out = nn(lhs, jnp.concatenate([ah, am, ah, al, am, ah], axis=0))
    sens_a = out[:16]
    sens_v = thirds(out[16:] - all_sums[16:])

    x = red_sum(3, x2_ref, x2_slots, across)
    x = unflattened([x[0:1], x[1:2]])
    y = solved(jnp.concatenate([x - mix_w, right], axis=0))[:, :COLS]
    yh, ym, yl = thirds(y)
    lhs = jnp.concatenate([yh, yh, ym, yh, ym, yl], axis=1)

    def finish(step, _):
        lanes = pl.ds(pl.multiple_of(step * 512, 512), 512)
        v = vp_ref[:, lanes]
        ah, am, al = v[0:16], v[16:32], v[32:48]
        out = nn(lhs, jnp.concatenate([ah, am, ah, al, am, ah], axis=0))
        adj_ref[:, lanes] = xa_ref[:, lanes] + out
        return 0

    lax.fori_loop(0, 8, finish, 0, unroll=8)
    ah, am, al = sens_v
    sens_ref[...] = sens_a + nn(lhs, jnp.concatenate([ah, am, ah, al, am, ah], axis=0))

    for d in range(6):
        end_face(d, zline)
        end_face(d, wline)
    red_all(0, g1_slots, along).wait_send()
    red_all(1, g2_slots, across).wait_send()
    red_all(2, x1_slots, along).wait_send()
    red_all(3, x2_slots, across).wait_send()
    carry.wait_send()


def on_device(sizes, loads, displacement, stiffness, col_index, face_index, zone_map):
    nx, ny, nz = sizes
    nb = ny * nz
    tiles = jnp.transpose(stiffness, (1, 0, 2)).reshape(7, 8, 8, 32, LANES)
    tiles = jnp.transpose(tiles, (0, 1, 3, 2, 4)).reshape(7 * 8 * 32 * 8, LANES)
    vmem = pl.BlockSpec(memory_space=pltpu.VMEM)
    dma = pltpu.SemaphoreType.DMA
    v = pltpu.VMEM
    return pl.pallas_call(
        functools.partial(kernel, sizes),
        out_shape=(
            jax.ShapeDtypeStruct((COLS, NODES * DOF), F32),
            jax.ShapeDtypeStruct((COLS, ZONE_DEV), F32),
        ),
        in_specs=[pl.BlockSpec(memory_space=pl.ANY)] * 6,
        out_specs=(vmem, vmem),
        scratch_shapes=[
            v((COLS, NODES * DOF), F32), v((32, LANES), F32), pltpu.SMEM((7, NODES), jnp.int32),
            pltpu.SMEM((6, 16), jnp.int32), v((6, NODES), jnp.int32),
            v((7 * 8 * 32 * 8, LANES), F32), v((2 * NODES * DOF, 512), BF16),
            v((EXT, COLS, LANES), F32), v((EXT, COLS, LANES), BF16), v((EXT, COLS, LANES), BF16),
            v((EXT, COLS, LANES), F32), v((EXT, COLS, LANES), BF16), v((EXT, COLS, LANES), BF16),
            v((COLS, NODES * DOF), F32), v((GROUPS * COLS, 256), F32),
            v((COLS, NODES * DOF), F32), v((COLS, NODES * DOF), F32),
            v((3 * COLS, NODES * DOF), BF16), v((COLS, NODES * DOF), F32),
            v((NODES, LANES), F32), v((32, LANES), F32), v((32, LANES), F32),
            v((EXT, LANES), F32), v((NODES * 8, LANES), F32),
            v((2 * NODES * 8, 256), BF16), v((2 * NODES * 8, 256), BF16), v((NODES, COLS, 256), F32),
            v((COLS, 3 * 1024), F32), v((2 * ZONE_DEV, 512), BF16), v((2 * COLS, 512), F32), v((256, 256), BF16),
            v((6, FACE_ROWS, LANES), F32), v((6, 8 * COLS, LANES), F32),
            v((6, FACE_ROWS, LANES), F32), v((6, 8 * COLS, LANES), F32),
            v((8, LANES), F32), v((8, LANES), F32),
            v((nx - 1, 8, LANES), F32), v((nb - 1, 8, LANES), F32),
            v((2, LANES), F32), v((2, LANES), F32),
            v((nx - 1, 2, LANES), F32), v((nb - 1, 2, LANES), F32),
            v((2 * COLS, ZONE_DEV), F32), v((2 * COLS, ZONE_DEV), F32),
            dma((7,)), dma((5,)), dma((6,)), dma((6,)), dma((6,)), dma((6,)),
            dma((4,)), dma((4,)), dma((2,)),
        ],
        compiler_params=pltpu.CompilerParams(
            collective_id=0, has_side_effects=True, vmem_limit_bytes=63 * 1024 * 1024
        ),
        cost_estimate=pl.CostEstimate(
            flops=400_000_000, bytes_accessed=8_000_000, transcendentals=0
        ),
    )(
        loads, displacement.reshape(32, LANES), tiles,
        jnp.transpose(col_index), face_index, jnp.transpose(zone_map),
    )


def solution(mesh):
    sizes = (mesh.shape["gx"], mesh.shape["gy"], mesh.shape["gz"])
    axes = ("gx", "gy", "gz")
    in_specs = (
        P(None, axes), P(axes), P(axes, None, None), P(axes, None), P(axes, None), P(axes, None),
    )
    return jax.shard_map(
        functools.partial(on_device, sizes), mesh=mesh, in_specs=in_specs,
        out_specs=(P(None, axes), P(None, axes)), check_vma=False,
    )
```

```python
import functools

import jax
import jax.numpy as jnp
from jax import lax
from jax.experimental import pallas as pl
from jax.experimental.pallas import tpu as pltpu
from jax.sharding import PartitionSpec as P

MESH = pl.DeviceIdType.MESH
F32 = jnp.float32
BF16 = jnp.bfloat16
NODES = 64
DOF = 64
COLS = 16
LANES = 128
GROUPS = 16
EXT = 160
ZONE_DEV = 128
PAIRS = ((0, 2), (4, 6), (1, 3), (5, None))
FACE_ROWS = 8 * COLS + 8


def nt(a, b):
    return lax.dot_general(a, b, (((1,), (1,)), ((), ())), preferred_element_type=F32)


def nn(a, b):
    return lax.dot_general(a, b, (((1,), (0,)), ((), ())), preferred_element_type=F32)


def exact_nn(a, b):
    return lax.dot_general(
        a, b, (((1,), (0,)), ((), ())), preferred_element_type=F32, precision=lax.Precision.HIGHEST
    )


def exact_nt(a, b):
    return lax.dot_general(
        a, b, (((1,), (1,)), ((), ())), preferred_element_type=F32, precision=lax.Precision.HIGHEST
    )


def halves(x):
    high = x.astype(BF16)
    return high, (x - high.astype(F32)).astype(BF16)


def thirds(x):
    high = x.astype(BF16)
    rest = x - high.astype(F32)
    mid = rest.astype(BF16)
    return high, mid, (rest - mid.astype(F32)).astype(BF16)


def iota(shape, dim):
    return lax.broadcasted_iota(jnp.int32, shape, dim)


def lower(rows=COLS):
    return iota((rows, LANES), 1) < DOF


def kernel(
    sizes,
    loads_in, disp_in, stiff_ref, col_in, face_in, zone_in,
    adj_ref, sens_ref,
    loads_ref, disp_ref, col_ref, face_ref, zone_ref,
    m_ref, w_ref,
    zf, zh, zl, wf, wh0, wl0,
    zp_ref, qs_ref, qp_ref, wp_ref, vp_ref,
    dinv_ref, dpack_ref, dsplit_ref, dext_ref, dd_ref,
    mm_ref, mv_ref, pushed_ref, out_ref, oh_ref, term_ref, perm_ref,
    zsend, wsend, zrecv, wrecv,
    g1_ref, g2_ref, g1_slots, g2_slots,
    part_ref, carry_ref,
    load_sems, input_sems, z_send_sems, z_recv_sems, w_send_sems, w_recv_sems,
    red_send_sems, red_recv_sems, carry_sems,
):
    nx, ny, nz = sizes
    nb = ny * nz
    mx, my, mz = lax.axis_index("gx"), lax.axis_index("gy"), lax.axis_index("gz")
    mb = my * nz + mz
    me = mx * nb + mb
    total = nx * nb

    def along(i):
        return (lax.rem(mx + i, nx), my, mz)

    def across(i):
        b = lax.rem(mb + i, nb)
        return (mx, b // nz, lax.rem(b, nz))

    def flat(i):
        s = lax.rem(me + i + total, total)
        b = lax.rem(s, nb)
        return (s // nb, b // nz, lax.rem(b, nz))

    rows_k = NODES // 8 * 32 * 8

    def stiff_copy(k):
        part = pl.ds(k * rows_k, rows_k)
        return pltpu.make_async_copy(stiff_ref.at[part], m_ref.at[part], load_sems.at[k])

    inputs = [
        pltpu.make_async_copy(a, b, input_sems.at[i])
        for i, (a, b) in enumerate((
            (loads_in, loads_ref), (disp_in, disp_ref), (face_in, face_ref), (zone_in, zone_ref),
            (col_in, col_ref),
        ))
    ]
    stiff_copy(0).start()
    for copy in inputs:
        copy.start()
    for pair in PAIRS:
        for k in pair:
            if k:
                stiff_copy(k).start()

    barrier = pltpu.get_barrier_semaphore()
    for i in range(1, nx):
        pl.semaphore_signal(barrier, inc=1, device_id=along(i), device_id_type=MESH)
    for i in range(1, nb):
        pl.semaphore_signal(barrier, inc=1, device_id=across(i), device_id_type=MESH)
    pl.semaphore_signal(barrier, inc=1, device_id=flat(-1), device_id_type=MESH)

    lo16, lo8, lo32 = lower(), lower(8), lower(32)

    prow, pcol = iota((256, 256), 0), iota((256, 256), 1)
    perm_ref[...] = jnp.where(
        (prow // DOF == pcol // DOF)
        & ((prow % DOF) // 32 + 2 * (prow % 32) == pcol % DOF),
        1.0, 0.0,
    ).astype(BF16)

    wh0[NODES:] = jnp.zeros((EXT - NODES, COLS, LANES), BF16)
    wl0[NODES:] = jnp.zeros((EXT - NODES, COLS, LANES), BF16)

    def put_rows(base, count, packed):
        turned = pltpu.roll(packed, DOF, 1)
        low = lower(count)
        dext_ref[pl.ds(base, count, stride=2), :] = jnp.where(low, packed, turned)
        dext_ref[pl.ds(base + 1, count, stride=2), :] = jnp.where(low, turned, packed)

    inputs[1].wait()
    put_rows(0, 32, disp_ref[...])

    inputs[3].wait()
    rel = lax.rem(zone_ref[...] - me * ZONE_DEV + total * ZONE_DEV, total * ZONE_DEV).astype(F32)
    rel = jnp.concatenate([jnp.zeros((1, NODES), F32), rel, jnp.zeros((1, NODES), F32)], axis=0)
    spread = jnp.where(iota((NODES, 512), 1) // 8 == iota((NODES, 512), 0), 1.0, 0.0).astype(BF16)
    spots = nn(rel.astype(BF16), spread)
    mine = iota((8, 512), 1) % 8 == iota((8, 512), 0)
    spot = jnp.sum(jnp.where(mine, spots, 0.0), axis=0, keepdims=True)
    entry = iota((1, 512), 1) % 8
    spot = jnp.where((entry == 0) | (entry == 7), -1.0, spot)
    for part in range(0, 2 * ZONE_DEV, 32):
        zone = (iota((32, 512), 0) + part).astype(F32)
        oh_ref[part : part + 32, :] = jnp.where(zone == spot, 1.0, 0.0).astype(BF16)

    stiff_copy(0).wait()
    lane8 = iota((8, LANES), 1)
    key = jnp.where(lane8 < DOF, lane8, lane8 - DOF)
    own = (key % 2 == 0) == (lane8 < DOF)
    key = jnp.where(own, key // 2, -1)

    def take_diagonal(quarter, _):
        got = [jnp.zeros((8, LANES), F32)] * 4
        for t in range(32):
            hit = key == t
            for i in range(4):
                base = pl.multiple_of(quarter * 1024, 1024)
                got[i] = jnp.where(hit, m_ref[pl.ds(base + i * 256 + t * 8, 8), :], got[i])
        for i in range(4):
            both = jnp.where(own, got[i], pltpu.roll(got[i], DOF, 1))
            rows = pl.ds(pl.multiple_of(quarter * 32, 32) + i * 8, 8)
            dinv_ref[rows, :] = 1.0 / both
        return 0

    lax.fori_loop(0, 2, take_diagonal, 0)
    dpack_ref[...] = jnp.where(
        lo32, dinv_ref[pl.ds(0, 32, stride=2), :], dinv_ref[pl.ds(1, 32, stride=2), :]
    )
    dhi, dmid, dlo = thirds(dpack_ref[...])
    small = perm_ref[:LANES, :LANES]
    dsplit_ref[...] = nt(dhi, small) + nt(dmid, small) + nt(dlo, small)

    def put_nodes(tile, node, full, high, low):
        turned = pltpu.roll(tile, DOF, 1)
        for i, x in enumerate((jnp.where(lo16, tile, turned), jnp.where(lo16, turned, tile))):
            full[node + i] = x
            xh, xl = halves(x)
            high[node + i] = xh
            low[node + i] = xl

    def put_full(tile, node, full):
        turned = pltpu.roll(tile, DOF, 1)
        full[node] = jnp.where(lo16, tile, turned)
        full[node + 1] = jnp.where(lo16, turned, tile)

    def start_z(tau, _):
        lanes = pl.ds(pl.multiple_of(tau * LANES, LANES), LANES)
        tile = loads_ref[:, lanes] * dpack_ref[pl.ds(tau, 1), :]
        zp_ref[:, lanes] = tile
        put_nodes(tile, 2 * tau, zf, zh, zl)
        return 0

    inputs[0].wait()
    lax.fori_loop(0, 32, start_z, 0, unroll=32)

    def fill_face(d, full, buf):
        for q in range(8):
            a, b = face_ref[d, 2 * q], face_ref[d, 2 * q + 1]
            buf[d, q * COLS : (q + 1) * COLS, :] = jnp.where(lo16, full[a], full[b])

    def fill_disp(d, buf):
        got = jnp.zeros((8, LANES), F32)
        sub = iota((8, LANES), 0)
        for q in range(8):
            a, b = face_ref[d, 2 * q], face_ref[d, 2 * q + 1]
            pair = jnp.where(lower(1), dext_ref[pl.ds(a, 1), :], dext_ref[pl.ds(b, 1), :])
            got = jnp.where(sub == q, jnp.broadcast_to(pair, (8, LANES)), got)
        buf[d, 8 * COLS : FACE_ROWS, :] = got

    place = (mx, mx, my, my, mz, mz)
    counts = (nx, nx, ny, ny, nz, nz)

    def has(d):
        return place[d] > 0 if d % 2 == 0 else place[d] < counts[d] - 1

    def neighbour(d):
        step = -1 if d % 2 == 0 else 1
        there = lax.rem(place[d] + step + counts[d], counts[d])
        return ((there, my, mz), (mx, there, mz), (mx, my, there))[d // 2]

    def face_copy(d, send, recv, send_sems, recv_sems):
        return pltpu.make_async_remote_copy(
            src_ref=send.at[d], dst_ref=recv.at[d ^ 1],
            send_sem=send_sems.at[d], recv_sem=recv_sems.at[d ^ 1],
            device_id=neighbour(d), device_id_type=MESH,
        )

    def face_arrival(d, send, recv, send_sems, recv_sems):
        return pltpu.make_async_remote_copy(
            src_ref=send.at[d], dst_ref=recv.at[d],
            send_sem=send_sems.at[d], recv_sem=recv_sems.at[d],
            device_id=neighbour(d), device_id_type=MESH,
        )

    zline = (zsend, zrecv, z_send_sems, z_recv_sems)
    wline = (wsend, wrecv, w_send_sems, w_recv_sems)

    inputs[2].wait()
    for d in range(6):
        fill_face(d, zf, zsend)
        fill_disp(d, zsend)

    pl.semaphore_wait(barrier, nx - 1 + nb - 1 + 1)

    def send_face(d, line):
        @pl.when(has(d))
        def _():
            face_copy(d, *line).start()

    def await_face(d, line):
        @pl.when(has(d))
        def _():
            face_arrival(d, *line).wait_recv()

        @pl.when(jnp.logical_not(has(d)))
        def _():
            line[1][d] = jnp.zeros(line[1].shape[1:], F32)

    def end_face(d, line):
        @pl.when(has(d))
        def _():
            face_copy(d, *line).wait_send()

    for d in range(6):
        send_face(d, zline)

    for at, (first, second) in enumerate(PAIRS):
        for k in (first, second):
            if k:
                stiff_copy(k).wait()

        def relay(octet, _, first=first, second=second, at=at):
            for s in range(8):
                base = pl.multiple_of((first * 8 + octet) * 256, 256)
                a = m_ref[pl.ds(base + s, 32, stride=8), :]
                if second is None:
                    b = jnp.zeros((32, LANES), F32)
                else:
                    base = pl.multiple_of((second * 8 + octet) * 256, 256)
                    b = m_ref[pl.ds(base + s, 32, stride=8), :]
                turned = pltpu.roll(jnp.where(lo32, b, a), DOF, 1)
                for p, x in enumerate((jnp.where(lo32, a, turned), jnp.where(lo32, turned, b))):
                    xh, xl = halves(x)
                    row = pl.multiple_of(octet * 1024, 1024) + (s // 4) * 512 + (s % 4) * DOF + p * 32
                    w_ref[pl.ds(row, 32), at * LANES : (at + 1) * LANES] = xh
                    w_ref[pl.ds(row + 256, 32), at * LANES : (at + 1) * LANES] = xl
            return 0

        lax.fori_loop(0, 8, relay, 0, unroll=8)

    def take_face(d, line, full, high, low):
        recv = line[1]
        for q in range(8):
            put_nodes(recv[d, q * COLS : (q + 1) * COLS, :], NODES + d * 16 + 2 * q, full, high, low)

    inputs[4].wait()
    for d in range(6):
        await_face(d, zline)
    for d in range(6):
        take_face(d, zline, zf, zh, zl)
        put_rows(NODES + d * 16, 8, zrecv[d, 8 * COLS : FACE_ROWS, :])

    def gathered(group, source):
        rows = []
        for r4 in range(4):
            r = group * 4 + r4
            parts = []
            for first, second in PAIRS:
                a = source[col_ref[first, r]]
                b = jnp.zeros_like(a) if second is None else source[col_ref[second, r]]
                parts.append(jnp.where(lo16, a, b))
            rows.append(jnp.concatenate(parts, axis=1))
        return jnp.concatenate(rows, axis=0)

    def own_part(x):
        return jnp.concatenate(
            [
                jnp.where(lo16, x[0:16, :LANES], x[16:32, :LANES]),
                jnp.where(lo16, x[32:48, LANES:], x[48:64, LANES:]),
            ],
            axis=1,
        )

    sub8 = iota((8, LANES), 0)
    def image(group, _):
        rows = pl.ds(pl.multiple_of(group * 512, 512), 512)
        left = jnp.concatenate([gathered(group, zh), gathered(group, zl)], axis=0)
        out = nt(left, w_ref[rows, :])
        out = out[:64, :256] + (out[64:, :256] + (out[:64, 256:] + out[64:, 256:]))
        qs_ref[pl.ds(pl.multiple_of(group * COLS, COLS), COLS), :] = own_part(out)
        return 0

    lax.fori_loop(0, GROUPS, image, 0, unroll=16)

    def natural(group, _):
        rows = pl.ds(pl.multiple_of(group * 64, 64), 64)
        hi, mid, lo = thirds(qs_ref[rows, :])
        out = nn(jnp.concatenate([hi, mid, lo], axis=0), perm_ref[...])
        out = out[:64] + out[64:128] + out[128:]
        for i in range(4):
            for h in range(2):
                tau = group * 8 + i * 2 + h
                lanes = pl.ds(pl.multiple_of(tau * LANES, LANES), LANES)
                tile = out[i * COLS : (i + 1) * COLS, h * LANES : (h + 1) * LANES]
                qp_ref[:, lanes] = tile
                tile = tile * dpack_ref[pl.ds(tau, 1), :]
                wp_ref[:, lanes] = tile
                put_nodes(tile, 2 * tau, wf, wh0, wl0)
        return 0

    lax.fori_loop(0, 4, natural, 0, unroll=4)

    for d in (0, 2, 4, 1, 3, 5):
        fill_face(d, wf, wsend)
        send_face(d, wline)

    def split_w(group, _):
        rows = pl.ds(pl.multiple_of(group * COLS, COLS), COLS)
        by = [dsplit_ref[pl.ds(group * 2 + h, 1), :] for h in range(2)]
        qs_ref[rows, :] = qs_ref[rows, :] * jnp.concatenate(by, axis=1)
        return 0

    lax.fori_loop(0, GROUPS, split_w, 0, unroll=4)

    def gram(left, right):
        n, m = left.shape[0], right.shape[0]
        out = nt(jnp.concatenate(halves(left), axis=0), jnp.concatenate(halves(right), axis=0))
        return out[:n, :m] + (out[n:, :m] + (out[:n, m:] + out[n:, m:]))

    def product(step, sums):
        lanes = pl.ds(pl.multiple_of(step * 512, 512), 512)
        z, q, w = zp_ref[:, lanes], qp_ref[:, lanes], wp_ref[:, lanes]
        n0 = gram(loads_ref[:, lanes], z)
        cw = gram(jnp.concatenate([z, w], axis=0), q)
        return sums[0] + n0, sums[1] + cw[:16], sums[2] + cw[16:]

    zero16 = jnp.zeros((COLS, COLS), F32)
    grams = lax.fori_loop(0, 8, product, (zero16, zero16, zero16), unroll=8)

    row16, lane16 = iota((COLS, LANES), 0), iota((COLS, LANES), 1)
    fits16 = row16 % 8 == lane16 // 16
    fits8 = sub8 == lane8 // 16

    def repeated(x):
        x = jnp.concatenate([x, jnp.zeros((COLS, LANES - COLS), F32)], axis=1)
        for by in (16, 32, 64):
            x = x + pltpu.roll(x, by, 1)
        return x

    def flattened(x):
        x = jnp.where(fits16, repeated(x), 0.0)
        return [jnp.sum(x[0:8], axis=0, keepdims=True), jnp.sum(x[8:16], axis=0, keepdims=True)]

    def unflattened(rows):
        out = []
        for row in rows:
            x = jnp.where(fits8, jnp.broadcast_to(row, (8, LANES)), 0.0)
            for by in (16, 32, 64):
                x = x + pltpu.roll(x, by, 1)
            out.append(x)
        return jnp.concatenate(out, axis=0)

    def red_copy(i, stage, src, slots, peer):
        return pltpu.make_async_remote_copy(
            src_ref=src, dst_ref=slots.at[i - 1],
            send_sem=red_send_sems.at[stage], recv_sem=red_recv_sems.at[stage],
            device_id=peer(i), device_id_type=MESH,
        )

    def red_all(stage, slots, peer):
        return pltpu.make_async_remote_copy(
            src_ref=slots, dst_ref=slots,
            send_sem=red_send_sems.at[stage], recv_sem=red_recv_sems.at[stage],
            device_id=peer(1), device_id_type=MESH,
        )

    def red_send(stage, src, slots, peer, count):
        for i in range(1, count):
            red_copy(i, stage, src, slots, peer).start()

    def red_sum(stage, src, slots, peer):
        red_all(stage, slots, peer).wait_recv()
        got = [src[...]] + [slots[i] for i in range(slots.shape[0])]
        while len(got) > 1:
            got = [a + b for a, b in zip(got[::2], got[1::2])] + got[len(got) & ~1 :]
        return got[0]

    half = jnp.where(lo16, 0.5, 1.0)
    block256 = iota((COLS, 256), 1) // DOF

    def push(group, _):
        w = qs_ref[pl.ds(pl.multiple_of(group * COLS, COLS), COLS), :]
        left = jnp.concatenate([jnp.where(block256 == i, w, 0.0) for i in range(4)], axis=0)
        base = pl.multiple_of(group * 512, 512)
        left = jnp.concatenate(halves(left), axis=0)
        a = nn(left, w_ref[pl.ds(base, 256), :256])
        b = nn(left, w_ref[pl.ds(pl.multiple_of(base + 256, 256), 256), :256])
        out = a[:64] + (a[64:] + (b[:64] + b[64:]))
        for i in range(4):
            rows = out[i * COLS : (i + 1) * COLS]
            pushed_ref[group * 4 + i, :, :LANES] = rows[:, :LANES] * half
            pushed_ref[group * 4 + i, :, LANES:] = rows[:, LANES:]
        return 0

    lax.fori_loop(0, GROUPS, push, 0, unroll=8)

    def within(step, total_):
        left, high, low = [], [], []
        for i in range(4):
            r = step * 4 + i
            left.append(pushed_ref[r])
            for first, second in PAIRS[:2]:
                a, b = col_ref[first, r], col_ref[second, r]
                high.append(jnp.where(lo16, wh0[a], wh0[b]))
                low.append(jnp.where(lo16, wl0[a], wl0[b]))
        left = jnp.concatenate(halves(jnp.concatenate(left, axis=1)), axis=0)
        right = jnp.concatenate([jnp.concatenate(high, axis=1), jnp.concatenate(low, axis=1)], axis=0)
        out = nt(left, right)
        return total_ + out[:16, :16] + (out[16:, :16] + (out[:16, 16:] + out[16:, 16:]))

    inside = lax.fori_loop(0, GROUPS, within, zero16, unroll=16)
    unit = jnp.where(iota((COLS, COLS), 0) == iota((COLS, COLS), 1), 1.0, 0.0)
    inside = inside + exact_nt(unit, inside)

    rows = flattened(grams[0]) + flattened(grams[1]) + flattened(grams[2])
    packed_early = jnp.zeros((8, LANES), F32)
    for i, row in enumerate(rows):
        packed_early = jnp.where(sub8 == i, jnp.broadcast_to(row, (8, LANES)), packed_early)

    for at, (d, tile, upper) in enumerate(((1, 0, True), (3, 1, False), (5, 1, True))):
        for q in range(8):
            a = pushed_ref[face_ref[d, 2 * q], :, tile * LANES : (tile + 1) * LANES]
            b = pushed_ref[face_ref[d, 2 * q + 1], :, tile * LANES : (tile + 1) * LANES]
            x = jnp.where(lo16, pltpu.roll(a, DOF, 1), b) if upper else jnp.where(lo16, a, pltpu.roll(b, DOF, 1))
            out_ref[:, (at * 8 + q) * LANES : (at * 8 + q + 1) * LANES] = x

    for d in (1, 3, 5):
        await_face(d, wline)
    curved = inside
    for at, d in enumerate((1, 3, 5)):
        there = jnp.concatenate([wrecv[d, q * COLS : (q + 1) * COLS, :] for q in range(8)], axis=1)
        here = out_ref[:, at * 1024 : (at + 1) * 1024]
        curved = curved + (gram(here, there) + gram(there, here))
    packed = packed_early
    for i, row in enumerate(flattened(curved)):
        packed = jnp.where(sub8 == 6 + i, jnp.broadcast_to(row, (8, LANES)), packed)
    g1_ref[...] = packed
    red_send(0, g1_ref, g1_slots, along, nx)

    def differ(r, _):
        got = jnp.zeros((8, LANES), F32)
        for k in range(1, 7):
            there = jnp.broadcast_to(dext_ref[pl.ds(col_ref[k, r], 1), :], (8, LANES))
            here = jnp.broadcast_to(dext_ref[pl.ds(r, 1), :], (8, LANES))
            got = jnp.where(sub8 == k, here - there, got)
        dd_ref[pl.ds(pl.multiple_of(r * 8, 8), 8), :] = got
        return 0

    lax.fori_loop(0, NODES, differ, 0, unroll=16)

    k32, lane32 = iota((32, LANES), 0) % 8, iota((32, LANES), 1)
    fit256 = iota((32, 256), 0) // 8 == iota((32, 256), 1) // DOF

    def moved(group, _):
        small = pl.ds(pl.multiple_of(group * 32, 32), 32)
        d = dd_ref[small, :]
        parts = []
        for first, second in PAIRS:
            keep = (k32 == first) & (lane32 < DOF)
            if second is not None:
                keep = keep | ((k32 == second) & (lane32 >= DOF))
            parts.append(jnp.where(keep, d, 0.0))
        left = jnp.concatenate(halves(jnp.concatenate(parts, axis=1)), axis=0)
        out = nt(left, w_ref[pl.ds(pl.multiple_of(group * 512, 512), 512), :])
        out = out[:32, :256] + (out[32:, :256] + (out[:32, 256:] + out[32:, 256:]))
        hi, lo = halves(jnp.where(fit256, out, 0.0))
        row = pl.multiple_of((group // 2) * 128, 128) + (group % 2) * 32
        mm_ref[pl.ds(pl.multiple_of(row, 32), 32), :] = hi
        mm_ref[pl.ds(pl.multiple_of(row + 64, 32), 32), :] = lo
        return 0

    lax.fori_loop(0, GROUPS, moved, 0, unroll=16)

    def moved_natural(four, _):
        rows = pl.ds(pl.multiple_of(four * 256, 256), 256)
        mv_ref[rows, :] = nn(mm_ref[rows, :], perm_ref[...]).astype(BF16)
        return 0

    lax.fori_loop(0, 4, moved_natural, 0, unroll=4)

    g2_ref[...] = red_sum(0, g1_ref, g1_slots, along)
    red_send(1, g2_ref, g2_slots, across, nb)


    pair_at, kind = iota((COLS, LANES), 1) // 32 % 2, iota((COLS, LANES), 1) % 8

    def terms(four, base, full):
        pairs = []
        for pair in range(2):
            weights = mv_ref[pl.ds(pl.multiple_of(four * 256, 256) + pair * 128, 128), :]
            got = jnp.zeros((COLS, LANES), F32)
            for g in range(2):
                r = (four * 4 + pair * 2 + g) * 4
                here = [jnp.where(lo16, full[r + 2 * h], full[r + 2 * h + 1]) for h in range(2)]
                parts = []
                for k in range(1, 7):
                    there = [
                        jnp.where(lo16, full[col_ref[k, r + 2 * h]], full[col_ref[k, r + 2 * h + 1]])
                        for h in range(2)
                    ]
                    parts.append(jnp.concatenate([here[h] - there[h] for h in range(2)], axis=1))
                hi, lo = halves(jnp.concatenate(parts, axis=0))
                out = nt(jnp.concatenate([hi, lo], axis=0), weights)
                out = out[:96] + out[96:]
                for k in range(1, 7):
                    keep = (pair_at == g) & (kind == k)
                    got = jnp.where(keep, out[(k - 1) * COLS : k * COLS], got)
            pairs.append(got + pltpu.roll(got, DOF, 1))
        lanes = pl.ds(pl.multiple_of(four * LANES, LANES), LANES)
        term_ref[base : base + COLS, lanes] = 0.5 * jnp.where(lo16, pairs[0], pairs[1])

    def terms_z(four, _):
        terms(four, 0, zf)
        return 0

    def terms_w(four, _):
        terms(four, COLS, wf)
        return 0


    lax.fori_loop(0, 4, terms_z, 0, unroll=4)

    for d in (0, 2, 4):
        await_face(d, wline)
    for d in range(6):
        for q in range(8):
            put_full(wrecv[d, q * COLS : (q + 1) * COLS, :], NODES + d * 16 + 2 * q, wf)
    lax.fori_loop(0, 4, terms_w, 0, unroll=4)

    hi, mid, lo = thirds(term_ref[...])
    sums = nt(jnp.concatenate([hi, mid, lo], axis=0), oh_ref[...])
    sums = sums[:32] + sums[32:64] + sums[64:]
    own_sums = sums[:, :ZONE_DEV]
    part_ref[...] = sums[:, ZONE_DEV:]
    carry = pltpu.make_async_remote_copy(
        src_ref=part_ref, dst_ref=carry_ref, send_sem=carry_sems.at[0], recv_sem=carry_sems.at[1],
        device_id=flat(1), device_id_type=MESH,
    )
    carry.start()

    def stacked(z, w):
        ah, am, al = thirds(jnp.concatenate([z, w], axis=0))
        return jnp.concatenate([ah, am, ah, al, am, ah], axis=0)

    def prepare(step, _):
        lanes = pl.ds(pl.multiple_of(step * 512, 512), 512)
        vp_ref[:, lanes] = stacked(zp_ref[:, lanes], wp_ref[:, lanes])
        return 0

    lax.fori_loop(0, 8, prepare, 0, unroll=8)

    carry.wait_recv()
    all_sums = own_sums + carry_ref[...]
    sens_right = stacked(all_sums[:COLS], all_sums[COLS:])

    def solved(x, panel=16):
        n = x.shape[0]
        lane = iota((1, LANES), 1) % COLS
        for first in range(0, COLS, panel):
            cols = [
                jnp.broadcast_to(x[:, k : k + 1], (n, LANES)) for k in range(first, first + panel)
            ]
            for j in range(panel):
                k = first + j
                scaled = cols[j] * (1.0 / cols[j][k : k + 1, :])
                cols = [
                    scaled if i == j else c - scaled * c[k : k + 1, :] for i, c in enumerate(cols)
                ]
            new = x
            for j in range(panel):
                new = new - cols[j] * x[first + j : first + j + 1, :]
            for j in range(panel):
                new = jnp.where(lane == first + j, cols[j], new)
            x = new
        return x[COLS:]

    g = red_sum(1, g2_ref, g2_slots, across)
    n0 = unflattened([g[0:1], g[1:2]])
    c0 = unflattened([g[2:3], g[3:4]])
    w0 = unflattened([g[4:5], g[5:6]])
    first = solved(jnp.concatenate([c0, n0, w0], axis=0))
    step0, mix = first[:COLS], first[COLS:]
    low16 = lane16 < COLS
    step0_, mix_ = jnp.where(low16, step0, 0.0), jnp.where(low16, mix, 0.0)

    pad = jnp.zeros((LANES - COLS, LANES), F32)

    def times(a, b):
        return exact_nn(a, jnp.concatenate([b, pad], axis=0))

    mix_w = times(mix_, w0)
    right = times(step0_, w0) - c0

    x = unflattened([g[6:7], g[7:8]])
    y = solved(jnp.concatenate([x - mix_w, right], axis=0))
    y_ = jnp.where(low16, y, 0.0)
    both = jnp.concatenate([(step0 + times(y_, mix))[:, :COLS], -y[:, :COLS]], axis=1)
    yh, ym, yl = thirds(both)
    lhs = jnp.concatenate([yh, yh, ym, yh, ym, yl], axis=1)

    def finish(step, _):
        lanes = pl.ds(pl.multiple_of(step * 512, 512), 512)
        adj_ref[:, lanes] = nn(lhs, vp_ref[:, lanes])
        return 0

    lax.fori_loop(0, 8, finish, 0, unroll=8)
    sens_ref[...] = nn(lhs, sens_right)

    for d in range(6):
        end_face(d, zline)
        end_face(d, wline)
    red_all(0, g1_slots, along).wait_send()
    red_all(1, g2_slots, across).wait_send()
    carry.wait_send()


def settle(adj_in, sens_in, adj_out, sens_out, adj_ref, sens_ref, sems):
    pieces = [(sens_in, sens_ref, sens_out)]
    for i in range(2):
        for j in range(4):
            part = (pl.ds(i * 8, 8), pl.ds(j * 1024, 1024))
            pieces.append((adj_in.at[part], adj_ref.at[part], adj_out.at[part]))
    come = [pltpu.make_async_copy(a, b, sems.at[0, i]) for i, (a, b, _) in enumerate(pieces)]
    go = [pltpu.make_async_copy(b, c, sems.at[1, i]) for i, (_, b, c) in enumerate(pieces)]
    for copy in come:
        copy.start()
    for one, other in zip(come, go):
        one.wait()
        other.start()
    for copy in go:
        copy.wait()


def on_device(sizes, loads, displacement, stiffness, col_index, face_index, zone_map):
    nx, ny, nz = sizes
    nb = ny * nz
    tiles = jnp.transpose(stiffness, (1, 0, 2)).reshape(7, 8, 8, 32, LANES)
    tiles = jnp.transpose(tiles, (0, 1, 3, 2, 4)).reshape(7 * 8 * 32 * 8, LANES)
    vmem = pl.BlockSpec(memory_space=pltpu.VMEM)
    dma = pltpu.SemaphoreType.DMA
    v = pltpu.VMEM
    results = pl.pallas_call(
        functools.partial(kernel, sizes),
        out_shape=(
            jax.ShapeDtypeStruct((COLS, NODES * DOF), F32),
            jax.ShapeDtypeStruct((COLS, ZONE_DEV), F32),
        ),
        in_specs=[pl.BlockSpec(memory_space=pl.ANY)] * 6,
        out_specs=(vmem, vmem),
        scratch_shapes=[
            v((COLS, NODES * DOF), F32), v((32, LANES), F32), pltpu.SMEM((7, NODES), jnp.int32),
            pltpu.SMEM((6, 16), jnp.int32), v((6, NODES), jnp.int32),
            v((7 * 8 * 32 * 8, LANES), F32), v((2 * NODES * DOF, 512), BF16),
            v((EXT, COLS, LANES), F32), v((EXT, COLS, LANES), BF16), v((EXT, COLS, LANES), BF16),
            v((EXT, COLS, LANES), F32), v((EXT, COLS, LANES), BF16), v((EXT, COLS, LANES), BF16),
            v((COLS, NODES * DOF), F32), v((GROUPS * COLS, 256), F32),
            v((COLS, NODES * DOF), F32), v((COLS, NODES * DOF), F32),
            v((12 * COLS, NODES * DOF), BF16),
            v((NODES, LANES), F32), v((32, LANES), F32), v((32, LANES), F32),
            v((EXT, LANES), F32), v((NODES * 8, LANES), F32),
            v((2 * NODES * 8, 256), BF16), v((2 * NODES * 8, 256), BF16), v((NODES, COLS, 256), F32),
            v((COLS, 3 * 1024), F32), v((2 * ZONE_DEV, 512), BF16), v((2 * COLS, 512), F32), v((256, 256), BF16),
            v((6, FACE_ROWS, LANES), F32), v((6, 8 * COLS, LANES), F32),
            v((6, FACE_ROWS, LANES), F32), v((6, 8 * COLS, LANES), F32),
            v((8, LANES), F32), v((8, LANES), F32),
            v((nx - 1, 8, LANES), F32), v((nb - 1, 8, LANES), F32),
            v((2 * COLS, ZONE_DEV), F32), v((2 * COLS, ZONE_DEV), F32),
            dma((7,)), dma((5,)), dma((6,)), dma((6,)), dma((6,)), dma((6,)),
            dma((2,)), dma((2,)), dma((2,)),
        ],
        compiler_params=pltpu.CompilerParams(
            collective_id=0, has_side_effects=True, vmem_limit_bytes=63 * 1024 * 1024
        ),
        cost_estimate=pl.CostEstimate(
            flops=400_000_000, bytes_accessed=8_000_000, transcendentals=0
        ),
    )(
        loads, displacement.reshape(32, LANES), tiles,
        jnp.transpose(col_index), face_index, jnp.transpose(zone_map),
    )
    hbm = pl.BlockSpec(memory_space=pl.ANY)
    return pl.pallas_call(
        settle,
        out_shape=(
            jax.ShapeDtypeStruct((COLS, NODES * DOF), F32),
            jax.ShapeDtypeStruct((COLS, ZONE_DEV), F32),
        ),
        in_specs=[hbm, hbm],
        out_specs=(hbm, hbm),
        scratch_shapes=[v((COLS, NODES * DOF), F32), v((COLS, ZONE_DEV), F32), dma((2, 9))],
        compiler_params=pltpu.CompilerParams(vmem_limit_bytes=63 * 1024 * 1024),
    )(*results)


def solution(mesh):
    sizes = (mesh.shape["gx"], mesh.shape["gy"], mesh.shape["gz"])
    axes = ("gx", "gy", "gz")
    in_specs = (
        P(None, axes), P(axes), P(axes, None, None), P(axes, None), P(axes, None), P(axes, None),
    )
    return jax.shard_map(
        functools.partial(on_device, sizes), mesh=mesh, in_specs=in_specs,
        out_specs=(P(None, axes), P(None, axes)), check_vma=False,
    )
```

```python
import functools

import jax
import jax.numpy as jnp
from jax import lax
from jax.experimental import pallas as pl
from jax.experimental.pallas import tpu as pltpu
from jax.sharding import PartitionSpec as P

MESH = pl.DeviceIdType.MESH
F32 = jnp.float32
BF16 = jnp.bfloat16
NODES = 64
DOF = 64
COLS = 16
LANES = 128
GROUPS = 16
EXT = 160
ZONE_DEV = 128
PAIRS = ((0, 2), (4, 6), (1, 3), (5, None))
FACE_ROWS = 8 * COLS + 8


def nt(a, b):
    return lax.dot_general(a, b, (((1,), (1,)), ((), ())), preferred_element_type=F32)


def nn(a, b):
    return lax.dot_general(a, b, (((1,), (0,)), ((), ())), preferred_element_type=F32)


def exact_nn(a, b):
    return lax.dot_general(
        a, b, (((1,), (0,)), ((), ())), preferred_element_type=F32, precision=lax.Precision.HIGHEST
    )


def exact_nt(a, b):
    return lax.dot_general(
        a, b, (((1,), (1,)), ((), ())), preferred_element_type=F32, precision=lax.Precision.HIGHEST
    )


def halves(x):
    high = x.astype(BF16)
    return high, (x - high.astype(F32)).astype(BF16)


def thirds(x):
    high = x.astype(BF16)
    rest = x - high.astype(F32)
    mid = rest.astype(BF16)
    return high, mid, (rest - mid.astype(F32)).astype(BF16)


def iota(shape, dim):
    return lax.broadcasted_iota(jnp.int32, shape, dim)


def lower(rows=COLS):
    return iota((rows, LANES), 1) < DOF


def kernel(
    sizes,
    loads_in, disp_in, stiff_ref, col_in, face_in, zone_in,
    adj_out, sens_out,
    adj_ref, sens_ref, loads_ref, disp_ref, col_ref, face_ref, zone_ref,
    m_ref, w_ref,
    zf, zh, zl, wf, wh0, wl0,
    zp_ref, qs_ref, qp_ref, wp_ref, vp_ref,
    dinv_ref, dpack_ref, dsplit_ref, dext_ref, dd_ref,
    mm_ref, mv_ref, pushed_ref, out_ref, oh_ref, term_ref, perm_ref,
    zsend, wsend, zrecv, wrecv,
    g1_ref, g2_ref, g1_slots, g2_slots,
    part_ref, carry_ref,
    load_sems, input_sems, z_send_sems, z_recv_sems, w_send_sems, w_recv_sems,
    red_send_sems, red_recv_sems, carry_sems, out_sems,
):
    nx, ny, nz = sizes
    nb = ny * nz
    mx, my, mz = lax.axis_index("gx"), lax.axis_index("gy"), lax.axis_index("gz")
    mb = my * nz + mz
    me = mx * nb + mb
    total = nx * nb

    def along(i):
        return (lax.rem(mx + i, nx), my, mz)

    def across(i):
        b = lax.rem(mb + i, nb)
        return (mx, b // nz, lax.rem(b, nz))

    def flat(i):
        s = lax.rem(me + i + total, total)
        b = lax.rem(s, nb)
        return (s // nb, b // nz, lax.rem(b, nz))

    rows_k = NODES // 8 * 32 * 8

    def stiff_copy(k):
        part = pl.ds(k * rows_k, rows_k)
        return pltpu.make_async_copy(stiff_ref.at[part], m_ref.at[part], load_sems.at[k])

    inputs = [
        pltpu.make_async_copy(a, b, input_sems.at[i])
        for i, (a, b) in enumerate((
            (loads_in, loads_ref), (disp_in, disp_ref), (face_in, face_ref), (zone_in, zone_ref),
            (col_in, col_ref),
        ))
    ]
    stiff_copy(0).start()
    for copy in inputs:
        copy.start()
    for pair in PAIRS:
        for k in pair:
            if k:
                stiff_copy(k).start()

    barrier = pltpu.get_barrier_semaphore()
    for i in range(1, nx):
        pl.semaphore_signal(barrier, inc=1, device_id=along(i), device_id_type=MESH)
    for i in range(1, nb):
        pl.semaphore_signal(barrier, inc=1, device_id=across(i), device_id_type=MESH)
    pl.semaphore_signal(barrier, inc=1, device_id=flat(-1), device_id_type=MESH)

    lo16, lo8, lo32 = lower(), lower(8), lower(32)

    prow, pcol = iota((256, 256), 0), iota((256, 256), 1)
    perm_ref[...] = jnp.where(
        (prow // DOF == pcol // DOF)
        & ((prow % DOF) // 32 + 2 * (prow % 32) == pcol % DOF),
        1.0, 0.0,
    ).astype(BF16)

    wh0[NODES:] = jnp.zeros((EXT - NODES, COLS, LANES), BF16)
    wl0[NODES:] = jnp.zeros((EXT - NODES, COLS, LANES), BF16)

    def put_rows(base, count, packed):
        turned = pltpu.roll(packed, DOF, 1)
        low = lower(count)
        dext_ref[pl.ds(base, count, stride=2), :] = jnp.where(low, packed, turned)
        dext_ref[pl.ds(base + 1, count, stride=2), :] = jnp.where(low, turned, packed)

    inputs[1].wait()
    put_rows(0, 32, disp_ref[...])

    inputs[3].wait()
    rel = lax.rem(zone_ref[...] - me * ZONE_DEV + total * ZONE_DEV, total * ZONE_DEV).astype(F32)
    rel = jnp.concatenate([jnp.zeros((1, NODES), F32), rel, jnp.zeros((1, NODES), F32)], axis=0)
    spread = jnp.where(iota((NODES, 512), 1) // 8 == iota((NODES, 512), 0), 1.0, 0.0).astype(BF16)
    spots = nn(rel.astype(BF16), spread)
    mine = iota((8, 512), 1) % 8 == iota((8, 512), 0)
    spot = jnp.sum(jnp.where(mine, spots, 0.0), axis=0, keepdims=True)
    entry = iota((1, 512), 1) % 8
    spot = jnp.where((entry == 0) | (entry == 7), -1.0, spot)
    for part in range(0, 2 * ZONE_DEV, 32):
        zone = (iota((32, 512), 0) + part).astype(F32)
        oh_ref[part : part + 32, :] = jnp.where(zone == spot, 1.0, 0.0).astype(BF16)

    stiff_copy(0).wait()
    lane8 = iota((8, LANES), 1)
    key = jnp.where(lane8 < DOF, lane8, lane8 - DOF)
    own = (key % 2 == 0) == (lane8 < DOF)
    key = jnp.where(own, key // 2, -1)

    def take_diagonal(quarter, _):
        got = [jnp.zeros((8, LANES), F32)] * 4
        for t in range(32):
            hit = key == t
            for i in range(4):
                base = pl.multiple_of(quarter * 1024, 1024)
                got[i] = jnp.where(hit, m_ref[pl.ds(base + i * 256 + t * 8, 8), :], got[i])
        for i in range(4):
            both = jnp.where(own, got[i], pltpu.roll(got[i], DOF, 1))
            rows = pl.ds(pl.multiple_of(quarter * 32, 32) + i * 8, 8)
            dinv_ref[rows, :] = 1.0 / both
        return 0

    lax.fori_loop(0, 2, take_diagonal, 0)
    dpack_ref[...] = jnp.where(
        lo32, dinv_ref[pl.ds(0, 32, stride=2), :], dinv_ref[pl.ds(1, 32, stride=2), :]
    )
    dhi, dmid, dlo = thirds(dpack_ref[...])
    small = perm_ref[:LANES, :LANES]
    dsplit_ref[...] = nt(dhi, small) + nt(dmid, small) + nt(dlo, small)

    def put_nodes(tile, node, full, high, low):
        turned = pltpu.roll(tile, DOF, 1)
        for i, x in enumerate((jnp.where(lo16, tile, turned), jnp.where(lo16, turned, tile))):
            full[node + i] = x
            xh, xl = halves(x)
            high[node + i] = xh
            low[node + i] = xl

    def put_full(tile, node, full):
        turned = pltpu.roll(tile, DOF, 1)
        full[node] = jnp.where(lo16, tile, turned)
        full[node + 1] = jnp.where(lo16, turned, tile)

    def start_z(tau, _):
        lanes = pl.ds(pl.multiple_of(tau * LANES, LANES), LANES)
        tile = loads_ref[:, lanes] * dpack_ref[pl.ds(tau, 1), :]
        zp_ref[:, lanes] = tile
        put_nodes(tile, 2 * tau, zf, zh, zl)
        return 0

    inputs[0].wait()
    lax.fori_loop(0, 32, start_z, 0, unroll=32)

    def fill_face(d, full, buf):
        for q in range(8):
            a, b = face_ref[d, 2 * q], face_ref[d, 2 * q + 1]
            buf[d, q * COLS : (q + 1) * COLS, :] = jnp.where(lo16, full[a], full[b])

    def fill_disp(d, buf):
        got = jnp.zeros((8, LANES), F32)
        sub = iota((8, LANES), 0)
        for q in range(8):
            a, b = face_ref[d, 2 * q], face_ref[d, 2 * q + 1]
            pair = jnp.where(lower(1), dext_ref[pl.ds(a, 1), :], dext_ref[pl.ds(b, 1), :])
            got = jnp.where(sub == q, jnp.broadcast_to(pair, (8, LANES)), got)
        buf[d, 8 * COLS : FACE_ROWS, :] = got

    place = (mx, mx, my, my, mz, mz)
    counts = (nx, nx, ny, ny, nz, nz)

    def has(d):
        return place[d] > 0 if d % 2 == 0 else place[d] < counts[d] - 1

    def neighbour(d):
        step = -1 if d % 2 == 0 else 1
        there = lax.rem(place[d] + step + counts[d], counts[d])
        return ((there, my, mz), (mx, there, mz), (mx, my, there))[d // 2]

    def face_copy(d, send, recv, send_sems, recv_sems):
        return pltpu.make_async_remote_copy(
            src_ref=send.at[d], dst_ref=recv.at[d ^ 1],
            send_sem=send_sems.at[d], recv_sem=recv_sems.at[d ^ 1],
            device_id=neighbour(d), device_id_type=MESH,
        )

    def face_arrival(d, send, recv, send_sems, recv_sems):
        return pltpu.make_async_remote_copy(
            src_ref=send.at[d], dst_ref=recv.at[d],
            send_sem=send_sems.at[d], recv_sem=recv_sems.at[d],
            device_id=neighbour(d), device_id_type=MESH,
        )

    zline = (zsend, zrecv, z_send_sems, z_recv_sems)
    wline = (wsend, wrecv, w_send_sems, w_recv_sems)

    inputs[2].wait()
    for d in range(6):
        fill_face(d, zf, zsend)
        fill_disp(d, zsend)

    pl.semaphore_wait(barrier, nx - 1 + nb - 1 + 1)

    def send_face(d, line):
        @pl.when(has(d))
        def _():
            face_copy(d, *line).start()

    def await_face(d, line):
        @pl.when(has(d))
        def _():
            face_arrival(d, *line).wait_recv()

        @pl.when(jnp.logical_not(has(d)))
        def _():
            line[1][d] = jnp.zeros(line[1].shape[1:], F32)

    def end_face(d, line):
        @pl.when(has(d))
        def _():
            face_copy(d, *line).wait_send()

    for d in range(6):
        send_face(d, zline)

    for at, (first, second) in enumerate(PAIRS):
        for k in (first, second):
            if k:
                stiff_copy(k).wait()

        def relay(octet, _, first=first, second=second, at=at):
            for s in range(8):
                base = pl.multiple_of((first * 8 + octet) * 256, 256)
                a = m_ref[pl.ds(base + s, 32, stride=8), :]
                if second is None:
                    b = jnp.zeros((32, LANES), F32)
                else:
                    base = pl.multiple_of((second * 8 + octet) * 256, 256)
                    b = m_ref[pl.ds(base + s, 32, stride=8), :]
                turned = pltpu.roll(jnp.where(lo32, b, a), DOF, 1)
                for p, x in enumerate((jnp.where(lo32, a, turned), jnp.where(lo32, turned, b))):
                    xh, xl = halves(x)
                    row = pl.multiple_of(octet * 1024, 1024) + (s // 4) * 512 + (s % 4) * DOF + p * 32
                    w_ref[pl.ds(row, 32), at * LANES : (at + 1) * LANES] = xh
                    w_ref[pl.ds(row + 256, 32), at * LANES : (at + 1) * LANES] = xl
            return 0

        lax.fori_loop(0, 8, relay, 0, unroll=8)

    def take_face(d, line, full, high, low):
        recv = line[1]
        for q in range(8):
            put_nodes(recv[d, q * COLS : (q + 1) * COLS, :], NODES + d * 16 + 2 * q, full, high, low)

    inputs[4].wait()
    for d in range(6):
        await_face(d, zline)
    for d in range(6):
        take_face(d, zline, zf, zh, zl)
        put_rows(NODES + d * 16, 8, zrecv[d, 8 * COLS : FACE_ROWS, :])

    def gathered(group, source):
        rows = []
        for r4 in range(4):
            r = group * 4 + r4
            parts = []
            for first, second in PAIRS:
                a = source[col_ref[first, r]]
                b = jnp.zeros_like(a) if second is None else source[col_ref[second, r]]
                parts.append(jnp.where(lo16, a, b))
            rows.append(jnp.concatenate(parts, axis=1))
        return jnp.concatenate(rows, axis=0)

    def own_part(x):
        return jnp.concatenate(
            [
                jnp.where(lo16, x[0:16, :LANES], x[16:32, :LANES]),
                jnp.where(lo16, x[32:48, LANES:], x[48:64, LANES:]),
            ],
            axis=1,
        )

    sub8 = iota((8, LANES), 0)
    def image(group, _):
        rows = pl.ds(pl.multiple_of(group * 512, 512), 512)
        left = jnp.concatenate([gathered(group, zh), gathered(group, zl)], axis=0)
        out = nt(left, w_ref[rows, :])
        out = out[:64, :256] + (out[64:, :256] + (out[:64, 256:] + out[64:, 256:]))
        qs_ref[pl.ds(pl.multiple_of(group * COLS, COLS), COLS), :] = own_part(out)
        return 0

    lax.fori_loop(0, GROUPS, image, 0, unroll=16)

    def natural(group, _):
        rows = pl.ds(pl.multiple_of(group * 64, 64), 64)
        hi, mid, lo = thirds(qs_ref[rows, :])
        out = nn(jnp.concatenate([hi, mid, lo], axis=0), perm_ref[...])
        out = out[:64] + out[64:128] + out[128:]
        for i in range(4):
            for h in range(2):
                tau = group * 8 + i * 2 + h
                lanes = pl.ds(pl.multiple_of(tau * LANES, LANES), LANES)
                tile = out[i * COLS : (i + 1) * COLS, h * LANES : (h + 1) * LANES]
                qp_ref[:, lanes] = tile
                tile = tile * dpack_ref[pl.ds(tau, 1), :]
                wp_ref[:, lanes] = tile
                put_nodes(tile, 2 * tau, wf, wh0, wl0)
        return 0

    lax.fori_loop(0, 4, natural, 0, unroll=4)

    for d in (0, 2, 4, 1, 3, 5):
        fill_face(d, wf, wsend)
        send_face(d, wline)

    def split_w(group, _):
        rows = pl.ds(pl.multiple_of(group * COLS, COLS), COLS)
        by = [dsplit_ref[pl.ds(group * 2 + h, 1), :] for h in range(2)]
        qs_ref[rows, :] = qs_ref[rows, :] * jnp.concatenate(by, axis=1)
        return 0

    lax.fori_loop(0, GROUPS, split_w, 0, unroll=4)

    def gram(left, right):
        n, m = left.shape[0], right.shape[0]
        out = nt(jnp.concatenate(halves(left), axis=0), jnp.concatenate(halves(right), axis=0))
        return out[:n, :m] + (out[n:, :m] + (out[:n, m:] + out[n:, m:]))

    def product(step, sums):
        lanes = pl.ds(pl.multiple_of(step * 512, 512), 512)
        z, q, w = zp_ref[:, lanes], qp_ref[:, lanes], wp_ref[:, lanes]
        n0 = gram(loads_ref[:, lanes], z)
        cw = gram(jnp.concatenate([z, w], axis=0), q)
        return sums[0] + n0, sums[1] + cw[:16], sums[2] + cw[16:]

    zero16 = jnp.zeros((COLS, COLS), F32)
    grams = lax.fori_loop(0, 8, product, (zero16, zero16, zero16), unroll=8)

    row16, lane16 = iota((COLS, LANES), 0), iota((COLS, LANES), 1)
    fits16 = row16 % 8 == lane16 // 16
    fits8 = sub8 == lane8 // 16

    def repeated(x):
        x = jnp.concatenate([x, jnp.zeros((COLS, LANES - COLS), F32)], axis=1)
        for by in (16, 32, 64):
            x = x + pltpu.roll(x, by, 1)
        return x

    def flattened(x):
        x = jnp.where(fits16, repeated(x), 0.0)
        return [jnp.sum(x[0:8], axis=0, keepdims=True), jnp.sum(x[8:16], axis=0, keepdims=True)]

    def unflattened(rows):
        out = []
        for row in rows:
            x = jnp.where(fits8, jnp.broadcast_to(row, (8, LANES)), 0.0)
            for by in (16, 32, 64):
                x = x + pltpu.roll(x, by, 1)
            out.append(x)
        return jnp.concatenate(out, axis=0)

    def red_copy(i, stage, src, slots, peer):
        return pltpu.make_async_remote_copy(
            src_ref=src, dst_ref=slots.at[i - 1],
            send_sem=red_send_sems.at[stage], recv_sem=red_recv_sems.at[stage],
            device_id=peer(i), device_id_type=MESH,
        )

    def red_all(stage, slots, peer):
        return pltpu.make_async_remote_copy(
            src_ref=slots, dst_ref=slots,
            send_sem=red_send_sems.at[stage], recv_sem=red_recv_sems.at[stage],
            device_id=peer(1), device_id_type=MESH,
        )

    def red_send(stage, src, slots, peer, count):
        for i in range(1, count):
            red_copy(i, stage, src, slots, peer).start()

    def red_sum(stage, src, slots, peer):
        red_all(stage, slots, peer).wait_recv()
        got = [src[...]] + [slots[i] for i in range(slots.shape[0])]
        while len(got) > 1:
            got = [a + b for a, b in zip(got[::2], got[1::2])] + got[len(got) & ~1 :]
        return got[0]

    half = jnp.where(lo16, 0.5, 1.0)
    block256 = iota((COLS, 256), 1) // DOF

    def push(group, _):
        w = qs_ref[pl.ds(pl.multiple_of(group * COLS, COLS), COLS), :]
        left = jnp.concatenate([jnp.where(block256 == i, w, 0.0) for i in range(4)], axis=0)
        base = pl.multiple_of(group * 512, 512)
        left = jnp.concatenate(halves(left), axis=0)
        a = nn(left, w_ref[pl.ds(base, 256), :256])
        b = nn(left, w_ref[pl.ds(pl.multiple_of(base + 256, 256), 256), :256])
        out = a[:64] + (a[64:] + (b[:64] + b[64:]))
        for i in range(4):
            rows = out[i * COLS : (i + 1) * COLS]
            pushed_ref[group * 4 + i, :, :LANES] = rows[:, :LANES] * half
            pushed_ref[group * 4 + i, :, LANES:] = rows[:, LANES:]
        return 0

    lax.fori_loop(0, GROUPS, push, 0, unroll=8)

    def within(step, total_):
        left, high, low = [], [], []
        for i in range(4):
            r = step * 4 + i
            left.append(pushed_ref[r])
            for first, second in PAIRS[:2]:
                a, b = col_ref[first, r], col_ref[second, r]
                high.append(jnp.where(lo16, wh0[a], wh0[b]))
                low.append(jnp.where(lo16, wl0[a], wl0[b]))
        left = jnp.concatenate(halves(jnp.concatenate(left, axis=1)), axis=0)
        right = jnp.concatenate([jnp.concatenate(high, axis=1), jnp.concatenate(low, axis=1)], axis=0)
        out = nt(left, right)
        return total_ + out[:16, :16] + (out[16:, :16] + (out[:16, 16:] + out[16:, 16:]))

    inside = lax.fori_loop(0, GROUPS, within, zero16, unroll=16)
    unit = jnp.where(iota((COLS, COLS), 0) == iota((COLS, COLS), 1), 1.0, 0.0)
    inside = inside + exact_nt(unit, inside)

    rows = flattened(grams[0]) + flattened(grams[1]) + flattened(grams[2])
    packed_early = jnp.zeros((8, LANES), F32)
    for i, row in enumerate(rows):
        packed_early = jnp.where(sub8 == i, jnp.broadcast_to(row, (8, LANES)), packed_early)

    for at, (d, tile, upper) in enumerate(((1, 0, True), (3, 1, False), (5, 1, True))):
        for q in range(8):
            a = pushed_ref[face_ref[d, 2 * q], :, tile * LANES : (tile + 1) * LANES]
            b = pushed_ref[face_ref[d, 2 * q + 1], :, tile * LANES : (tile + 1) * LANES]
            x = jnp.where(lo16, pltpu.roll(a, DOF, 1), b) if upper else jnp.where(lo16, a, pltpu.roll(b, DOF, 1))
            out_ref[:, (at * 8 + q) * LANES : (at * 8 + q + 1) * LANES] = x

    for d in (1, 3, 5):
        await_face(d, wline)
    curved = inside
    for at, d in enumerate((1, 3, 5)):
        there = jnp.concatenate([wrecv[d, q * COLS : (q + 1) * COLS, :] for q in range(8)], axis=1)
        here = out_ref[:, at * 1024 : (at + 1) * 1024]
        curved = curved + (gram(here, there) + gram(there, here))
    packed = packed_early
    for i, row in enumerate(flattened(curved)):
        packed = jnp.where(sub8 == 6 + i, jnp.broadcast_to(row, (8, LANES)), packed)
    g1_ref[...] = packed
    red_send(0, g1_ref, g1_slots, along, nx)

    def differ(r, _):
        got = jnp.zeros((8, LANES), F32)
        for k in range(1, 7):
            there = jnp.broadcast_to(dext_ref[pl.ds(col_ref[k, r], 1), :], (8, LANES))
            here = jnp.broadcast_to(dext_ref[pl.ds(r, 1), :], (8, LANES))
            got = jnp.where(sub8 == k, here - there, got)
        dd_ref[pl.ds(pl.multiple_of(r * 8, 8), 8), :] = got
        return 0

    lax.fori_loop(0, NODES, differ, 0, unroll=16)

    k32, lane32 = iota((32, LANES), 0) % 8, iota((32, LANES), 1)
    fit256 = iota((32, 256), 0) // 8 == iota((32, 256), 1) // DOF

    def moved(group, _):
        small = pl.ds(pl.multiple_of(group * 32, 32), 32)
        d = dd_ref[small, :]
        parts = []
        for first, second in PAIRS:
            keep = (k32 == first) & (lane32 < DOF)
            if second is not None:
                keep = keep | ((k32 == second) & (lane32 >= DOF))
            parts.append(jnp.where(keep, d, 0.0))
        left = jnp.concatenate(halves(jnp.concatenate(parts, axis=1)), axis=0)
        out = nt(left, w_ref[pl.ds(pl.multiple_of(group * 512, 512), 512), :])
        out = out[:32, :256] + (out[32:, :256] + (out[:32, 256:] + out[32:, 256:]))
        hi, lo = halves(jnp.where(fit256, out, 0.0))
        row = pl.multiple_of((group // 2) * 128, 128) + (group % 2) * 32
        mm_ref[pl.ds(pl.multiple_of(row, 32), 32), :] = hi
        mm_ref[pl.ds(pl.multiple_of(row + 64, 32), 32), :] = lo
        return 0

    lax.fori_loop(0, GROUPS, moved, 0, unroll=16)

    def moved_natural(four, _):
        rows = pl.ds(pl.multiple_of(four * 256, 256), 256)
        mv_ref[rows, :] = nn(mm_ref[rows, :], perm_ref[...]).astype(BF16)
        return 0

    lax.fori_loop(0, 4, moved_natural, 0, unroll=4)

    g2_ref[...] = red_sum(0, g1_ref, g1_slots, along)
    red_send(1, g2_ref, g2_slots, across, nb)


    pair_at, kind = iota((COLS, LANES), 1) // 32 % 2, iota((COLS, LANES), 1) % 8

    def terms(four, base, full):
        pairs = []
        for pair in range(2):
            weights = mv_ref[pl.ds(pl.multiple_of(four * 256, 256) + pair * 128, 128), :]
            got = jnp.zeros((COLS, LANES), F32)
            for g in range(2):
                r = (four * 4 + pair * 2 + g) * 4
                here = [jnp.where(lo16, full[r + 2 * h], full[r + 2 * h + 1]) for h in range(2)]
                parts = []
                for k in range(1, 7):
                    there = [
                        jnp.where(lo16, full[col_ref[k, r + 2 * h]], full[col_ref[k, r + 2 * h + 1]])
                        for h in range(2)
                    ]
                    parts.append(jnp.concatenate([here[h] - there[h] for h in range(2)], axis=1))
                hi, lo = halves(jnp.concatenate(parts, axis=0))
                out = nt(jnp.concatenate([hi, lo], axis=0), weights)
                out = out[:96] + out[96:]
                for k in range(1, 7):
                    keep = (pair_at == g) & (kind == k)
                    got = jnp.where(keep, out[(k - 1) * COLS : k * COLS], got)
            pairs.append(got + pltpu.roll(got, DOF, 1))
        lanes = pl.ds(pl.multiple_of(four * LANES, LANES), LANES)
        term_ref[base : base + COLS, lanes] = 0.5 * jnp.where(lo16, pairs[0], pairs[1])

    def terms_z(four, _):
        terms(four, 0, zf)
        return 0

    def terms_w(four, _):
        terms(four, COLS, wf)
        return 0


    lax.fori_loop(0, 4, terms_z, 0, unroll=4)

    for d in (0, 2, 4):
        await_face(d, wline)
    for d in range(6):
        for q in range(8):
            put_full(wrecv[d, q * COLS : (q + 1) * COLS, :], NODES + d * 16 + 2 * q, wf)
    lax.fori_loop(0, 4, terms_w, 0, unroll=4)

    hi, mid, lo = thirds(term_ref[...])
    sums = nt(jnp.concatenate([hi, mid, lo], axis=0), oh_ref[...])
    sums = sums[:32] + sums[32:64] + sums[64:]
    own_sums = sums[:, :ZONE_DEV]
    part_ref[...] = sums[:, ZONE_DEV:]
    carry = pltpu.make_async_remote_copy(
        src_ref=part_ref, dst_ref=carry_ref, send_sem=carry_sems.at[0], recv_sem=carry_sems.at[1],
        device_id=flat(1), device_id_type=MESH,
    )
    carry.start()

    def stacked(z, w):
        ah, am, al = thirds(jnp.concatenate([z, w], axis=0))
        return jnp.concatenate([ah, am, ah, al, am, ah], axis=0)

    def prepare(step, _):
        lanes = pl.ds(pl.multiple_of(step * 512, 512), 512)
        vp_ref[:, lanes] = stacked(zp_ref[:, lanes], wp_ref[:, lanes])
        return 0

    lax.fori_loop(0, 8, prepare, 0, unroll=8)

    carry.wait_recv()
    all_sums = own_sums + carry_ref[...]
    sens_right = stacked(all_sums[:COLS], all_sums[COLS:])

    def solved(x, panel=16):
        n = x.shape[0]
        lane = iota((1, LANES), 1) % COLS
        for first in range(0, COLS, panel):
            cols = [
                jnp.broadcast_to(x[:, k : k + 1], (n, LANES)) for k in range(first, first + panel)
            ]
            for j in range(panel):
                k = first + j
                scaled = cols[j] * (1.0 / cols[j][k : k + 1, :])
                cols = [
                    scaled if i == j else c - scaled * c[k : k + 1, :] for i, c in enumerate(cols)
                ]
            new = x
            for j in range(panel):
                new = new - cols[j] * x[first + j : first + j + 1, :]
            for j in range(panel):
                new = jnp.where(lane == first + j, cols[j], new)
            x = new
        return x[COLS:]

    g = red_sum(1, g2_ref, g2_slots, across)
    n0 = unflattened([g[0:1], g[1:2]])
    c0 = unflattened([g[2:3], g[3:4]])
    w0 = unflattened([g[4:5], g[5:6]])
    first = solved(jnp.concatenate([c0, n0, w0], axis=0))
    step0, mix = first[:COLS], first[COLS:]
    low16 = lane16 < COLS
    step0_, mix_ = jnp.where(low16, step0, 0.0), jnp.where(low16, mix, 0.0)

    pad = jnp.zeros((LANES - COLS, LANES), F32)

    def times(a, b):
        return exact_nn(a, jnp.concatenate([b, pad], axis=0))

    mix_w = times(mix_, w0)
    right = times(step0_, w0) - c0

    x = unflattened([g[6:7], g[7:8]])
    y = solved(jnp.concatenate([x - mix_w, right], axis=0))
    y_ = jnp.where(low16, y, 0.0)
    both = jnp.concatenate([(step0 + times(y_, mix))[:, :COLS], -y[:, :COLS]], axis=1)
    yh, ym, yl = thirds(both)
    lhs = jnp.concatenate([yh, yh, ym, yh, ym, yl], axis=1)

    leaving = [pltpu.make_async_copy(sens_ref, sens_out, out_sems.at[8])]
    sens_ref[...] = nn(lhs, sens_right)
    leaving[0].start()
    for step in range(8):
        lanes = pl.ds(step * 512, 512)
        adj_ref[:, lanes] = nn(lhs, vp_ref[:, lanes])
        copy = pltpu.make_async_copy(adj_ref.at[:, lanes], adj_out.at[:, lanes], out_sems.at[step])
        copy.start()
        leaving.append(copy)

    for d in range(6):
        end_face(d, zline)
        end_face(d, wline)
    red_all(0, g1_slots, along).wait_send()
    red_all(1, g2_slots, across).wait_send()
    carry.wait_send()
    for copy in leaving:
        copy.wait()


def settle(adj_in, sens_in, adj_out, sens_out, adj_ref, sens_ref, sems):
    pieces = [(sens_in, sens_ref, sens_out)]
    for i in range(2):
        for j in range(4):
            part = (pl.ds(i * 8, 8), pl.ds(j * 1024, 1024))
            pieces.append((adj_in.at[part], adj_ref.at[part], adj_out.at[part]))
    come = [pltpu.make_async_copy(a, b, sems.at[0, i]) for i, (a, b, _) in enumerate(pieces)]
    go = [pltpu.make_async_copy(b, c, sems.at[1, i]) for i, (_, b, c) in enumerate(pieces)]
    for copy in come:
        copy.start()
    for one, other in zip(come, go):
        one.wait()
        other.start()
    for copy in go:
        copy.wait()


def on_device(sizes, loads, displacement, stiffness, col_index, face_index, zone_map):
    nx, ny, nz = sizes
    nb = ny * nz
    tiles = jnp.transpose(stiffness, (1, 0, 2)).reshape(7, 8, 8, 32, LANES)
    tiles = jnp.transpose(tiles, (0, 1, 3, 2, 4)).reshape(7 * 8 * 32 * 8, LANES)
    dma = pltpu.SemaphoreType.DMA
    v = pltpu.VMEM
    results = pl.pallas_call(
        functools.partial(kernel, sizes),
        out_shape=(
            jax.ShapeDtypeStruct((COLS, NODES * DOF), F32),
            jax.ShapeDtypeStruct((COLS, ZONE_DEV), F32),
        ),
        in_specs=[pl.BlockSpec(memory_space=pl.ANY)] * 6,
        out_specs=(pl.BlockSpec(memory_space=pl.ANY),) * 2,
        scratch_shapes=[
            v((COLS, NODES * DOF), F32), v((COLS, ZONE_DEV), F32),
            v((COLS, NODES * DOF), F32), v((32, LANES), F32), pltpu.SMEM((7, NODES), jnp.int32),
            pltpu.SMEM((6, 16), jnp.int32), v((6, NODES), jnp.int32),
            v((7 * 8 * 32 * 8, LANES), F32), v((2 * NODES * DOF, 512), BF16),
            v((EXT, COLS, LANES), F32), v((EXT, COLS, LANES), BF16), v((EXT, COLS, LANES), BF16),
            v((EXT, COLS, LANES), F32), v((EXT, COLS, LANES), BF16), v((EXT, COLS, LANES), BF16),
            v((COLS, NODES * DOF), F32), v((GROUPS * COLS, 256), F32),
            v((COLS, NODES * DOF), F32), v((COLS, NODES * DOF), F32),
            v((12 * COLS, NODES * DOF), BF16),
            v((NODES, LANES), F32), v((32, LANES), F32), v((32, LANES), F32),
            v((EXT, LANES), F32), v((NODES * 8, LANES), F32),
            v((2 * NODES * 8, 256), BF16), v((2 * NODES * 8, 256), BF16), v((NODES, COLS, 256), F32),
            v((COLS, 3 * 1024), F32), v((2 * ZONE_DEV, 512), BF16), v((2 * COLS, 512), F32), v((256, 256), BF16),
            v((6, FACE_ROWS, LANES), F32), v((6, 8 * COLS, LANES), F32),
            v((6, FACE_ROWS, LANES), F32), v((6, 8 * COLS, LANES), F32),
            v((8, LANES), F32), v((8, LANES), F32),
            v((nx - 1, 8, LANES), F32), v((nb - 1, 8, LANES), F32),
            v((2 * COLS, ZONE_DEV), F32), v((2 * COLS, ZONE_DEV), F32),
            dma((7,)), dma((5,)), dma((6,)), dma((6,)), dma((6,)), dma((6,)),
            dma((2,)), dma((2,)), dma((2,)), dma((9,)),
        ],
        compiler_params=pltpu.CompilerParams(
            collective_id=0, has_side_effects=True, vmem_limit_bytes=63 * 1024 * 1024
        ),
        cost_estimate=pl.CostEstimate(
            flops=400_000_000, bytes_accessed=8_000_000, transcendentals=0
        ),
    )(
        loads, displacement.reshape(32, LANES), tiles,
        jnp.transpose(col_index), face_index, jnp.transpose(zone_map),
    )
    hbm = pl.BlockSpec(memory_space=pl.ANY)
    return pl.pallas_call(
        settle,
        out_shape=(
            jax.ShapeDtypeStruct((COLS, NODES * DOF), F32),
            jax.ShapeDtypeStruct((COLS, ZONE_DEV), F32),
        ),
        in_specs=[hbm, hbm],
        out_specs=(hbm, hbm),
        scratch_shapes=[v((COLS, NODES * DOF), F32), v((COLS, ZONE_DEV), F32), dma((2, 9))],
        compiler_params=pltpu.CompilerParams(vmem_limit_bytes=63 * 1024 * 1024),
    )(*results)


def solution(mesh):
    sizes = (mesh.shape["gx"], mesh.shape["gy"], mesh.shape["gz"])
    axes = ("gx", "gy", "gz")
    in_specs = (
        P(None, axes), P(axes), P(axes, None, None), P(axes, None), P(axes, None), P(axes, None),
    )
    return jax.shard_map(
        functools.partial(on_device, sizes), mesh=mesh, in_specs=in_specs,
        out_specs=(P(None, axes), P(None, axes)), check_vma=False,
    )
```
